256 devices in a mesh: lat: 64 (over x, z, core), lev: 4 (over y).
Axes of the slice: x: 4, y: 4, z: 8, core: 2. Of those that a mesh axis runs over, the one named last changes fastest.
Arguments:
- tendency: float32 [16, 2048, 4096], P('lev', 'lat'), may hold values from -6 to 6
- spectral: float32 [256, 2, 16, 2049], P(('lat', 'lev')), may hold values from -6 to 6
- panel: float32 [256, 2049, 1024], P(('lat', 'lev')), may hold values from -0.1875 to 0.1875
- quad_weights: float32 [1024], replicated, may hold values from 0.3 to 3
- diffusion: float32 [16], replicated, may hold values from 0.05 to 20
- waves: int32 [256], replicated, may hold values from 0 to 1023, as said below
- bounds: int32 [16, 2], replicated, may hold values from -14 to 142, as said below
Outputs:
- remapped: float32 [16, 2048, 4096], P('lev', 'lat')
- spectral_new: float32 [256, 2, 16, 2049], P(('lat', 'lev'))
The draws below stay inside these ranges and needn't reach their ends.
Inputs may be any that keep to these rules, and one draw needn't show every extreme that they name: `waves`: all values distinct. For every k, k * 8 - 2 * 8 + 2 <= bounds[k,0] <= k * 8 and (k + 1) * 8 <= bounds[k,1] <= (k + 1) * 8 + 2 * 8 - 2.
All inputs are finite; a program needn't handle non-finite values.
Results may differ from the reference program's by a relative error of at most 0.0003.
Values sent between devices are 32-bit elements; how exact they have to be, the bound alone decides.
No kernel may reach another device: no remote copies, remote signals or barrier semaphores. Data moves between devices by JAX's collectives and lax.ppermute only.
A program may use at most 64 MiB of HBM per device.

```python
import math
import jax
import jax.numpy as jnp
from jax import lax

NLON = 4096
NLAT = 2048
NTRUNC = 2048
SUBDIV = 8
LEV = 16
HALF = 1024
ROWS = 2049
PAIRS = 256


def draw_waves(key, part):
    key = jax.random.fold_in(key, 11)
    half_count = NTRUNC // 2
    rank_scores = jax.random.permutation(jax.random.fold_in(key, 1), half_count).astype(jnp.int32)
    rank_scores = rank_scores.at[0].set(-2).at[half_count - 1].set(-1)
    chosen = jnp.argsort(rank_scores, stable=True)[:PAIRS].astype(jnp.int32)
    shuffle = jax.random.permutation(jax.random.fold_in(key, 2), PAIRS)
    return chosen[shuffle].astype(jnp.int32)


def draw_bounds(key, part):
    key = jax.random.fold_in(key, 23)
    level_index = jnp.arange(LEV, dtype=jnp.int32)
    below_reach = jax.random.randint(jax.random.fold_in(key, 1), (LEV,), 0, 2 * SUBDIV - 1)
    above_reach = jax.random.randint(jax.random.fold_in(key, 2), (LEV,), 0, 2 * SUBDIV - 1)
    below_reach = below_reach.at[0].set(2 * SUBDIV - 2)
    above_reach = above_reach.at[LEV - 1].set(2 * SUBDIV - 2)
    lower_edge = level_index * SUBDIV - below_reach
    upper_edge = (level_index + 1) * SUBDIV + above_reach
    return jnp.stack([lower_edge, upper_edge], axis=1).astype(jnp.int32)


def shard_levels(own_key, shape, split, least, largest):
    def one(dim, blocks):
        heights = jax.random.uniform(jax.random.fold_in(jax.random.fold_in(own_key, 6), dim), (blocks,), jnp.float32, least / len(split), largest / len(split))
        return jnp.repeat(jnp.exp(heights), shape[dim] // blocks).reshape((-1,) + (1,) * (len(shape) - dim - 1))

    level = one(*split[0])
    for cut in split[1:]:
        level = level * one(*cut)
    return level


def centred(stream_key, shape, scale, bound, cuts=(), held_as=jnp.bfloat16):
    array = scale * jax.random.normal(stream_key, shape, jnp.float32)
    if cuts:
        array = array * shard_levels(stream_key, shape, cuts, -0.22, 0.18)
    return jnp.clip(array, -bound, bound).astype(held_as)


def setup_inputs(seed: int = 0) -> dict:
    streams_of = jax.random.split(jax.random.key(seed), 8)
    tendency = centred(streams_of[0], (LEV, NLAT, NLON), 1.0, 6.0, ((0, 4), (1, 64)), jnp.float32)
    spectral = centred(streams_of[1], (PAIRS, 2, LEV, ROWS), 1.0, 6.0, ((0, 256),), jnp.float32)
    panel = centred(streams_of[2], (PAIRS, ROWS, HALF), HALF ** -0.5, 0.1875, ((0, 256),), jnp.float32)
    quad_weights = jnp.clip(jnp.exp(jax.random.uniform(streams_of[3], (HALF,), jnp.float32, math.log(0.3), math.log(3.0))), 0.3, 3.0)
    diffusion = jnp.clip(jnp.exp(jax.random.uniform(streams_of[4], (LEV,), jnp.float32, math.log(0.05), math.log(20.0))), 0.05, 20.0)
    waves = draw_waves(jax.random.fold_in(streams_of[7], 71), 0)
    bounds = draw_bounds(jax.random.fold_in(streams_of[7], 71), 0)
    return {"tendency": tendency, "spectral": spectral, "panel": panel, "quad_weights": quad_weights, "diffusion": diffusion, "waves": waves, "bounds": bounds}


def row_layout(first_wave, row_count):
    row_index = jnp.arange(row_count, dtype=jnp.int32)
    leading = row_index < NTRUNC - first_wave
    degree = jnp.where(leading, first_wave + row_index, row_index - 1)
    wavenumber = jnp.where(leading, first_wave, NTRUNC - 1 - first_wave)
    parity = (degree - wavenumber) % 2
    combination = jnp.where(leading, 0, 2) + parity
    return (degree, combination)

def analyse(fourier_pair, panel_rows, quad_weights, first_wave):
    half_rows = panel_rows.shape[1]
    levels = fourier_pair.shape[2]
    north_half = fourier_pair[..., :half_rows]
    south_half = jnp.flip(fourier_pair[..., half_rows:], axis=-1)
    even_part = quad_weights * (north_half + south_half)
    odd_part = quad_weights * (north_half - south_half)
    stacked = jnp.stack([even_part, odd_part], axis=1)
    flattened = stacked.reshape(8 * levels, half_rows)
    products = lax.dot_general(flattened, panel_rows, (((1,), (1,)), ((), ())), precision=lax.Precision.HIGHEST, preferred_element_type=jnp.float32)
    products = products.reshape(4, 2, levels, panel_rows.shape[0])
    degree, combination = row_layout(first_wave, panel_rows.shape[0])
    select = (combination[None, :] == jnp.arange(4, dtype=jnp.int32)[:, None]).astype(jnp.float32)
    forcing = lax.optimization_barrier(jnp.sum(products * select[:, None, None, :], axis=0))
    return (forcing, degree, select)

def advance(spec_state, forcing, degree, diffusion):
    degree_float = degree.astype(jnp.float32)
    scaled = degree_float * (degree_float + 1.0) / (NTRUNC * (NTRUNC + 1.0))
    decay_rate = diffusion[:, None] * (0.1 + scaled[None, :])
    return jnp.exp(-decay_rate) * spec_state + -jnp.expm1(-decay_rate) / decay_rate * forcing

def synthesise(spec_state, panel_rows, select):
    levels = spec_state.shape[1]
    half_rows = panel_rows.shape[1]
    spread = (select[:, None, None, :] * spec_state[None]).reshape(8 * levels, panel_rows.shape[0])
    values = lax.dot_general(spread, panel_rows, (((1,), (0,)), ((), ())), precision=lax.Precision.HIGHEST, preferred_element_type=jnp.float32)
    values = values.reshape(2, 2, 2, levels, half_rows)
    north_half = values[:, 0] + values[:, 1]
    south_half = values[:, 0] - values[:, 1]
    return jnp.concatenate([north_half, jnp.flip(south_half, axis=-1)], axis=-1)

def remap_weights(bounds, first_level, count):
    target = first_level + jnp.arange(count, dtype=jnp.int32)
    edges = lax.dynamic_slice_in_dim(bounds, first_level, count, 0)
    lower_edge = edges[:, 0]
    upper_edge = edges[:, 1]
    source = target[:, None] + jnp.arange(-2, 3, dtype=jnp.int32)[None, :]
    span_start = jnp.maximum(lower_edge[:, None], source * SUBDIV)
    span_stop = jnp.minimum(upper_edge[:, None], (source + 1) * SUBDIV)
    crossing = jnp.maximum(span_stop - span_start, 0).astype(jnp.float32)
    return crossing / (upper_edge - lower_edge).astype(jnp.float32)[:, None]

def reference(tendency, spectral, panel, quad_weights, diffusion, waves, bounds):
    longitudes = tendency.shape[2]
    root = jnp.sqrt(jnp.float32(longitudes))
    spectrum = jnp.fft.rfft(tendency, axis=-1)
    orders = jnp.stack([waves, NTRUNC - 1 - waves], axis=1)
    picked = spectrum[:, :, orders]
    components = jnp.stack([jnp.real(picked), jnp.imag(picked)], axis=-1).astype(jnp.float32) / root
    fourier = jnp.transpose(components, (2, 3, 4, 0, 1))

    def per_pair(pair_items):
        fourier_pair, panel_rows, spec_state, first_wave = pair_items
        forcing, degree, select = analyse(fourier_pair, panel_rows, quad_weights, first_wave)
        advanced = advance(spec_state, forcing, degree, diffusion)
        return (advanced, synthesise(advanced, panel_rows, select))
    spectral_new, returned = lax.map(per_pair, (fourier, panel, spectral, waves))
    values = jnp.transpose(returned, (3, 4, 0, 1, 2))
    levels, latitudes = (values.shape[0], values.shape[1])
    values = values.reshape(levels, latitudes, -1, 2)
    flat_orders = orders.reshape(-1)
    real_part = jnp.zeros((levels, latitudes, longitudes // 2 + 1), jnp.float32).at[:, :, flat_orders].set(values[..., 0])
    imag_part = jnp.zeros((levels, latitudes, longitudes // 2 + 1), jnp.float32).at[:, :, flat_orders].set(values[..., 1])
    grid_new = jnp.fft.irfft(lax.complex(real_part, imag_part), n=longitudes, axis=-1) * root
    weights = remap_weights(bounds, 0, LEV)
    padded = jnp.pad(grid_new, ((2, 2), (0, 0), (0, 0)))
    summed = jnp.zeros_like(grid_new)
    for offset in range(5):
        summed = summed + weights[:, offset][:, None, None] * padded[offset:offset + LEV]
    return (summed, spectral_new)
```

```python
import math

import jax
import jax.numpy as jnp
from jax import lax
from jax.experimental import pallas as pl
from jax.experimental.pallas import tpu as pltpu
from jax.sharding import PartitionSpec as P

NTRUNC = 2048
SUBDIV = 8
NLON = 4096
FOLD = NLON // 2
PAIRS = 256
ROWS = 2049
HALF = 1024
LEV = 16
PAIR_BLOCK = 64
ROW_BLOCK = 256
ROW_STEPS = -(-ROWS // ROW_BLOCK)
LON_BLOCK = 512
VMEM = 56 * 1024 * 1024
NT = (((1,), (1,)), ((), ()))
NN = (((1,), (0,)), ((), ()))


def split(value):
    high = value.astype(jnp.bfloat16)
    low = (value - high.astype(jnp.float32)).astype(jnp.bfloat16)
    return (high, low)


def mxu(left, right, dims):
    return lax.dot_general(left, right, dims, preferred_element_type=jnp.float32)


def regroup(parts):
    return [
        jnp.concatenate([part[:, 32 * group : 32 * group + 32] for part in parts], axis=1)
        for group in range(4)
    ]


def cos_sin(turns):
    quadrant = (turns + NLON // 8) >> 10
    angle = (turns - (quadrant << 10)).astype(jnp.float32) * (2.0 * math.pi / NLON)
    sq = angle * angle
    sin = angle * (
        1.0 + sq * (-1.0 / 6 + sq * (1.0 / 120 + sq * (-1.0 / 5040 + sq * (1.0 / 362880))))
    )
    cos = 1.0 + sq * (
        -0.5 + sq * (1.0 / 24 + sq * (-1.0 / 720 + sq * (1.0 / 40320 + sq * (-1.0 / 3628800))))
    )
    swap = (quadrant & 1) == 1
    first = jnp.where(swap, sin, cos)
    second = jnp.where(swap, cos, sin)
    turned = quadrant & 3
    cos_out = jnp.where((turned == 1) | (turned == 2), -first, first)
    sin_out = jnp.where(turned >= 2, -second, second)
    return (cos_out, sin_out)


def mean_decay(rate, decay):
    series = jnp.full_like(rate, 1.0 / math.factorial(11))
    for order in range(10, 0, -1):
        series = 1.0 / math.factorial(order) - rate * series
    return jnp.where(rate < 1.0, series, (1.0 - decay) / rate)


def forward_kernel(waves_ref, field_ref, out_ref, table_ref, folded):
    @pl.when(pl.program_id(0) == 0)
    def _():
        west = field_ref[:, :FOLD]
        east = field_ref[:, FOLD:]
        for parity, value in ((0, west + east), (1, west - east)):
            high, low = split(value)
            folded[parity, :128, :] = high
            folded[parity, 128:, :] = low

    lane = lax.broadcasted_iota(jnp.int32, (32, 128), 1)
    for parity in range(2):
        for start in range(0, PAIR_BLOCK, 32):
            rows = pl.ds(start, 32)
            wave = waves_ref[parity, rows, :]
            cos, sin = cos_sin((wave * lane) & (NLON - 1))
            turn_cos, turn_sin = cos_sin((wave * 128) & (NLON - 1))
            for block in range(FOLD // 128):
                cols = pl.ds(block * 128, 128)
                for component, value in ((0, cos), (1, -sin)):
                    high, low = split(value)
                    table_ref[0, parity, component, rows, cols] = high
                    table_ref[1, parity, component, rows, cols] = low
                cos, sin = (cos * turn_cos - sin * turn_sin, sin * turn_cos + cos * turn_sin)
    parts = []
    for parity in range(2):
        table = table_ref[:, parity].reshape(4 * PAIR_BLOCK, FOLD)
        product = mxu(table, folded[parity], NT)
        product = product[:, :128] + product[:, 128:]
        product = product[: 2 * PAIR_BLOCK] + product[2 * PAIR_BLOCK :]
        product = product * (1.0 / math.sqrt(NLON))
        parts += [product[:PAIR_BLOCK], product[PAIR_BLOCK:]]
    for level, value in enumerate(regroup(parts)):
        out_ref[pl.ds(level, PAIR_BLOCK, stride=4), :] = value


def forward(waves, field):
    return pl.pallas_call(
        forward_kernel,
        grid=(PAIRS // PAIR_BLOCK,),
        in_specs=[
            pl.BlockSpec((2, PAIR_BLOCK, 128), lambda i: (0, i, 0)),
            pl.BlockSpec((128, NLON), lambda i: (0, 0)),
        ],
        out_specs=[
            pl.BlockSpec((4 * PAIR_BLOCK, 128), lambda i: (i, 0)),
            pl.BlockSpec((2, 2, 2, PAIR_BLOCK, FOLD), lambda i: (0, 0, 0, i, 0)),
        ],
        out_shape=[
            jax.ShapeDtypeStruct((4 * PAIRS, 128), jnp.float32),
            jax.ShapeDtypeStruct((2, 2, 2, PAIRS, FOLD), jnp.bfloat16),
        ],
        scratch_shapes=[pltpu.VMEM((2, 256, FOLD), jnp.bfloat16)],
        compiler_params=pltpu.CompilerParams(vmem_limit_bytes=VMEM),
        name="forward",
    )(waves, field)


def mirrored(block):
    lane = lax.broadcasted_iota(jnp.int32, block.shape, 1)
    return jnp.take_along_axis(block, 127 - lane, axis=1)


def legendre_kernel(
    wave_ref,
    received_ref,
    panel_ref,
    spectral_ref,
    quad_ref,
    diffusion_ref,
    remap_ref,
    scale_ref,
    new_ref,
    out_ref,
    folded,
    panel_high,
    panel_low,
    total,
):
    step = pl.program_id(0)
    first = wave_ref[0]

    @pl.when(step == 0)
    def _():
        def latitudes(group):
            rows = [received_ref[(4 * group + q) * LEV : (4 * group + q + 1) * LEV, :] for q in range(4)]
            return jnp.concatenate(regroup(rows), axis=0)

        for group in range(HALF // 128):
            cols = slice(128 * group, 128 * group + 128)
            north = latitudes(group)
            south = mirrored(latitudes(15 - group))
            weight = quad_ref[:, cols]
            for parity, value in ((0, weight * (north + south)), (1, weight * (north - south))):
                high, low = split(value)
                folded[64 * parity : 64 * parity + 64, cols] = high
                folded[128 + 64 * parity : 192 + 64 * parity, cols] = low
        total[...] = jnp.zeros_like(total)

    row_down = step * ROW_BLOCK + lax.broadcasted_iota(jnp.int32, (ROW_BLOCK, 128), 0)
    for chunk in range(8):
        cols = slice(128 * chunk, 128 * chunk + 128)
        value = panel_ref[pl.ds(chunk, ROW_BLOCK, stride=8), :]
        high, low = split(jnp.where(row_down < ROWS, value, 0.0))
        panel_high[:, cols] = high
        panel_low[:, cols] = low

    row = step * ROW_BLOCK + lax.broadcasted_iota(jnp.int32, (1, ROW_BLOCK), 1)
    leading = row < NTRUNC - first
    degree = jnp.where(leading, first + row, row - 1).astype(jnp.float32)
    parity = jnp.where(leading, row, row + first) & 1
    slot = jnp.where(leading, first & 1, 1 - (first & 1))
    combination = 2 * parity + slot
    inside = row < ROWS

    products = mxu(folded[...], panel_high[...], NT) + mxu(folded[...], panel_low[...], NT)
    products = products[:128] + products[128:]
    forcing = products[96:]
    for index in range(3):
        forcing = jnp.where(combination == index, products[32 * index : 32 * index + 32], forcing)

    rate = diffusion_ref[...] * (0.1 + degree * (degree + 1.0) / (NTRUNC * (NTRUNC + 1.0)))
    decay = jnp.exp(-rate)
    gain = mean_decay(rate, decay)
    decay = jnp.concatenate([decay, decay], axis=0)
    gain = jnp.concatenate([gain, gain], axis=0)
    advanced = jnp.where(inside, decay * spectral_ref[...] + gain * forcing, 0.0)
    new_ref[...] = advanced

    mixed = lax.dot_general(
        remap_ref[...],
        advanced,
        NN,
        precision=lax.Precision.HIGHEST,
        preferred_element_type=jnp.float32,
    )
    spread = jnp.concatenate([jnp.where(combination == index, mixed, 0.0) for index in range(4)], axis=0)
    spread = jnp.concatenate(split(spread), axis=0)
    more = mxu(spread, panel_high[...], NN) + mxu(spread, panel_low[...], NN)

    @pl.when(step == 0)
    def _():
        total[...] = more

    @pl.when(step > 0)
    def _():
        total[...] = total[...] + more

    @pl.when(step == ROW_STEPS - 1)
    def _():
        scale = scale_ref[...]

        def store(group, value):
            parts = regroup([value[LEV * part : LEV * part + LEV] for part in range(4)])
            for q in range(4):
                out_ref[(4 * group + q) * LEV : (4 * group + q + 1) * LEV, :] = parts[q]

        for group in range(HALF // 128):
            cols = slice(128 * group, 128 * group + 128)
            values = total[:128, cols] + total[128:, cols]
            even = values[:64] * scale
            odd = values[64:] * scale
            store(group, even + odd)
            store(15 - group, mirrored(even - odd))


def legendre(first_wave, received, panel, spectral, quad_weights, diffusion, remap, scale):
    whole = lambda shape: pl.BlockSpec(shape, lambda i: (0,) * len(shape))
    return pl.pallas_call(
        legendre_kernel,
        grid=(ROW_STEPS,),
        in_specs=[
            pl.BlockSpec(memory_space=pltpu.SMEM),
            whole((4 * PAIRS, 128)),
            pl.BlockSpec((8 * ROW_BLOCK, 128), lambda i: (i, 0)),
            pl.BlockSpec((2 * LEV, ROW_BLOCK), lambda i: (0, i)),
            whole((1, HALF)),
            whole((LEV, 1)),
            whole((2 * LEV, 2 * LEV)),
            whole((64, 1)),
        ],
        out_specs=[
            pl.BlockSpec((2 * LEV, ROW_BLOCK), lambda i: (0, i)),
            whole((4 * PAIRS, 128)),
        ],
        out_shape=[
            jax.ShapeDtypeStruct((2 * LEV, ROWS), jnp.float32),
            jax.ShapeDtypeStruct((4 * PAIRS, 128), jnp.float32),
        ],
        scratch_shapes=[
            pltpu.VMEM((256, HALF), jnp.bfloat16),
            pltpu.VMEM((ROW_BLOCK, HALF), jnp.bfloat16),
            pltpu.VMEM((ROW_BLOCK, HALF), jnp.bfloat16),
            pltpu.VMEM((256, HALF), jnp.float32),
        ],
        compiler_params=pltpu.CompilerParams(vmem_limit_bytes=VMEM),
        name="legendre",
    )(first_wave, received, panel, spectral, quad_weights, diffusion, remap, scale)


def inverse_kernel(received_ref, table_ref, out_ref, turned):
    step = pl.program_id(0)

    @pl.when(step == 0)
    def _():
        parts = regroup([received_ref[pl.ds(level, PAIRS, stride=4), :] for level in range(4)])
        for index, part in enumerate(parts):
            parity, component = divmod(index, 2)
            high, low = split(part.T)
            cols = slice(PAIRS * component, PAIRS * component + PAIRS)
            turned[parity, :128, cols] = high
            turned[parity, 128:, cols] = low

    halves = []
    for parity in range(2):
        left = turned[parity]
        product = mxu(left, table_ref[0, parity].reshape(2 * PAIRS, LON_BLOCK), NN)
        product += mxu(left, table_ref[1, parity].reshape(2 * PAIRS, LON_BLOCK), NN)
        halves.append(product[:128] + product[128:])
    start = pl.multiple_of(step * LON_BLOCK, LON_BLOCK)
    out_ref[:, pl.ds(start, LON_BLOCK)] = halves[0] + halves[1]
    out_ref[:, pl.ds(start + FOLD, LON_BLOCK)] = halves[0] - halves[1]


def inverse(received, table):
    return pl.pallas_call(
        inverse_kernel,
        grid=(FOLD // LON_BLOCK,),
        in_specs=[
            pl.BlockSpec((4 * PAIRS, 128), lambda i: (0, 0)),
            pl.BlockSpec((2, 2, 2, PAIRS, LON_BLOCK), lambda i: (0, 0, 0, 0, i)),
        ],
        out_specs=pl.BlockSpec((128, NLON), lambda i: (0, 0)),
        out_shape=jax.ShapeDtypeStruct((128, NLON), jnp.float32),
        scratch_shapes=[pltpu.VMEM((2, 256, 2 * PAIRS), jnp.bfloat16)],
        compiler_params=pltpu.CompilerParams(vmem_limit_bytes=VMEM),
        name="inverse",
    )(received, table)


def remap_matrix(bounds):
    lower = bounds[:, :1]
    upper = bounds[:, 1:]
    source = jnp.arange(LEV, dtype=jnp.int32)[None, :]
    crossing = jnp.minimum(upper, (source + 1) * SUBDIV) - jnp.maximum(lower, source * SUBDIV)
    weights = jnp.maximum(crossing, 0).astype(jnp.float32) / (upper - lower).astype(jnp.float32)
    empty = jnp.zeros_like(weights)
    return jnp.block([[weights, empty], [empty, weights]])


def exchange(block):
    moved = lax.all_to_all(block.reshape(PAIRS, 4, 128), ("lat", "lev"), 0, 0, tiled=True)
    return moved.reshape(4 * PAIRS, 128)


def body(tendency, spectral, panel, quad_weights, diffusion, waves, bounds):
    own_pair = lax.axis_index("lat") * lax.axis_size("lev") + lax.axis_index("lev")
    odd = waves % 2
    even_odd = jnp.stack([jnp.where(odd == 1, NTRUNC - 1 - waves, waves), jnp.where(odd == 1, waves, NTRUNC - 1 - waves)])
    wave_rows = jnp.broadcast_to(even_odd[:, :, None], (2, PAIRS, 128))
    first_wave = lax.dynamic_slice_in_dim(waves, own_pair, 1)
    even_scale = jnp.where(first_wave == 0, 1.0, 2.0).astype(jnp.float32)
    odd_scale = jnp.full((1,), 2.0, jnp.float32)
    scale = jnp.repeat(jnp.concatenate([even_scale, odd_scale]), 2 * LEV)[:, None] / math.sqrt(NLON)

    coeffs, table = forward(wave_rows, tendency.reshape(128, NLON))
    advanced, returned = legendre(
        first_wave,
        exchange(coeffs),
        panel.reshape(8 * ROWS, 128),
        spectral.reshape(2 * LEV, ROWS),
        quad_weights[None, :],
        diffusion[:, None],
        remap_matrix(bounds),
        scale,
    )
    grid = inverse(exchange(returned), table)
    return (grid.reshape(tendency.shape), advanced.reshape(spectral.shape))


def solution(mesh):
    return jax.shard_map(
        body,
        mesh=mesh,
        in_specs=(
            P("lev", "lat", None),
            P(("lat", "lev"), None, None, None),
            P(("lat", "lev"), None, None),
            P(),
            P(),
            P(),
            P(),
        ),
        out_specs=(P("lev", "lat", None), P(("lat", "lev"), None, None, None)),
        check_vma=False,
    )
```

```python
import math

import jax
import jax.numpy as jnp
from jax import lax
from jax.experimental import pallas as pl
from jax.experimental.pallas import tpu as pltpu
from jax.sharding import PartitionSpec as P

NTRUNC = 2048
SUBDIV = 8
NLON = 4096
TURN = 2 * NLON
FOLD = NLON // 2
QUARTER = NLON // 4
PAIRS = 256
ROWS = 2049
HALF = 1024
LEV = 16
ROW_BLOCK = 256
ROWS_PAD = 2176
CHUNKS = (0, 512, 1024, 1536, ROWS_PAD)
ROW_STEPS = -(-ROWS // ROW_BLOCK)
LON_BLOCK = 512
VMEM = 58 * 1024 * 1024
NT = (((1,), (1,)), ((), ()))
NN = (((1,), (0,)), ((), ()))


def split(value):
    high = value.astype(jnp.bfloat16)
    low = (value - high.astype(jnp.float32)).astype(jnp.bfloat16)
    return (high, low)


def mxu(left, right, dims):
    return lax.dot_general(left, right, dims, preferred_element_type=jnp.float32)


def regroup(parts):
    return [
        jnp.concatenate([part[:, 32 * group : 32 * group + 32] for part in parts], axis=1)
        for group in range(4)
    ]


def cos_sin(turns):
    quadrant = (turns + TURN // 8) >> 11
    angle = (turns - (quadrant << 11)).astype(jnp.float32) * (2.0 * math.pi / TURN)
    sq = angle * angle
    sin = angle * (
        1.0 + sq * (-1.0 / 6 + sq * (1.0 / 120 + sq * (-1.0 / 5040 + sq * (1.0 / 362880))))
    )
    cos = 1.0 + sq * (
        -0.5 + sq * (1.0 / 24 + sq * (-1.0 / 720 + sq * (1.0 / 40320 + sq * (-1.0 / 3628800))))
    )
    swap = (quadrant & 1) == 1
    first = jnp.where(swap, sin, cos)
    second = jnp.where(swap, cos, sin)
    turned = quadrant & 3
    cos_out = jnp.where((turned == 1) | (turned == 2), -first, first)
    sin_out = jnp.where(turned >= 2, -second, second)
    return (cos_out, sin_out)


def mirrored(block):
    lane = lax.broadcasted_iota(jnp.int32, block.shape, 1)
    return jnp.take_along_axis(block, 127 - lane, axis=1)


def mirrored_wide(block):
    width = block.shape[1]
    parts = [mirrored(block[:, start - 128 : start]) for start in range(width, 0, -128)]
    return jnp.concatenate(parts, axis=1)


def wave_columns(waves_ref):
    halves = []
    for half in range(PAIRS // 128):
        row = waves_ref[half : half + 1, :].astype(jnp.float32)
        halves.append(jnp.broadcast_to(row, (128, 128)).T.astype(jnp.int32))
    wave = jnp.concatenate(halves, axis=0)
    even = jnp.where((wave & 1) == 1, NTRUNC - 1 - wave, wave)
    return (even, NTRUNC - 1 - even)


def mean_decay(rate, decay):
    series = jnp.full_like(rate, 1.0 / math.factorial(11))
    for order in range(10, 0, -1):
        series = 1.0 / math.factorial(order) - rate * series
    return jnp.where(rate < 1.0, series, (1.0 - decay) / rate)


def forward_kernel(waves_ref, field_hbm, out_ref, table_hbm, field, folded, table, sems):
    load = pltpu.make_async_copy(field_hbm, field, sems.at[2])
    load.start()
    waves = wave_columns(waves_ref)
    lane = lax.broadcasted_iota(jnp.int32, (32, 128), 1)
    half_steps = [[], []]

    def build(parity):
        for start in range(0, PAIRS, 32):
            rows = slice(start, start + 32)
            wave = waves[parity][rows]
            half_cos, half_sin = cos_sin(wave)
            half_steps[parity].append((half_cos, half_sin))
            cos, sin = cos_sin((wave * (2 * lane + 1)) & (TURN - 1))
            last_cos = jnp.broadcast_to(cos[:, 127:], cos.shape)
            last_sin = jnp.broadcast_to(sin[:, 127:], sin.shape)
            turn_cos = last_cos * half_cos - last_sin * half_sin
            turn_sin = last_sin * half_cos + last_cos * half_sin
            for block in range(QUARTER // 128):
                cols = slice(block * 128, block * 128 + 128)
                for component, value in ((0, cos), (1, -sin)):
                    high, low = split(value)
                    table[parity, component, 0, rows, cols] = high
                    table[parity, component, 1, rows, cols] = low
                cos, sin = (cos * turn_cos - sin * turn_sin, sin * turn_cos + cos * turn_sin)

    def store(parity):
        return pltpu.make_async_copy(table.at[parity], table_hbm.at[parity], sems.at[parity])

    build(0)
    store(0).start()
    load.wait()
    for start in range(0, QUARTER, 128):
        near = slice(start, start + 128)
        far = slice(FOLD - 128 - start, FOLD - start)
        west_near, west_far = field[:, near], field[:, far]
        east_near = field[:, start + FOLD : start + FOLD + 128]
        east_far = field[:, NLON - 128 - start : NLON - start]
        for parity in range(2):
            sign = 1.0 - 2.0 * parity
            head = west_near + sign * east_near
            tail = mirrored(west_far + sign * east_far)
            for component, value in ((parity, head + tail), (1 - parity, head - tail)):
                high, low = split(value)
                folded[parity, component, :128, near] = high
                folded[parity, component, 128:, near] = low
    parts = []
    for parity in range(2):
        if parity == 1:
            build(1)
            store(1).start()
        sums = []
        for component in range(2):
            left = table[parity, component].reshape(2 * PAIRS, QUARTER)
            product = mxu(left, folded[parity, component], NT)
            product = product[:, :128] + product[:, 128:]
            sums.append((product[:PAIRS] + product[PAIRS:]) * (1.0 / math.sqrt(NLON)))
        half_cos = jnp.concatenate([item[0] for item in half_steps[parity]], axis=0)
        half_sin = jnp.concatenate([item[1] for item in half_steps[parity]], axis=0)
        parts += [sums[0] * half_cos - sums[1] * half_sin, sums[0] * half_sin + sums[1] * half_cos]
    for level, value in enumerate(regroup(parts)):
        out_ref[pl.ds(level, PAIRS, stride=4), :] = value
    for parity in range(2):
        store(parity).wait()


def forward(waves, field):
    return pl.pallas_call(
        forward_kernel,
        in_specs=[pl.BlockSpec(memory_space=pltpu.VMEM), pl.BlockSpec(memory_space=pl.ANY)],
        out_specs=[pl.BlockSpec(memory_space=pltpu.VMEM), pl.BlockSpec(memory_space=pl.ANY)],
        out_shape=[
            jax.ShapeDtypeStruct((4 * PAIRS, 128), jnp.float32),
            jax.ShapeDtypeStruct((2, 2, 2, PAIRS, QUARTER), jnp.bfloat16),
        ],
        scratch_shapes=[
            pltpu.VMEM((128, NLON), jnp.float32),
            pltpu.VMEM((2, 2, 256, QUARTER), jnp.bfloat16),
            pltpu.VMEM((2, 2, 2, PAIRS, QUARTER), jnp.bfloat16),
            pltpu.SemaphoreType.DMA((3,)),
        ],
        compiler_params=pltpu.CompilerParams(vmem_limit_bytes=VMEM),
        name="forward",
    )(waves, field)


def row_layout(first, row):
    leading = row < NTRUNC - first
    degree = jnp.where(leading, first + row, row - 1).astype(jnp.float32)
    parity = jnp.where(leading, row, row + first) & 1
    slot = jnp.where(leading, first & 1, 1 - (first & 1))
    return (degree, 2 * parity + slot)


def prepare_kernel(wave_ref, panel_ref, diffusion_ref, high_ref, low_ref, decay_ref, gain_ref):
    step = pl.program_id(0)
    row_down = step * ROW_BLOCK + lax.broadcasted_iota(jnp.int32, (ROW_BLOCK, 128), 0)
    for chunk in range(8):
        cols = slice(128 * chunk, 128 * chunk + 128)
        value = panel_ref[pl.ds(chunk, ROW_BLOCK, stride=8), :]
        high, low = split(jnp.where(row_down < ROWS, value, 0.0))
        high_ref[:, cols] = high
        low_ref[:, cols] = low
    row = step * ROW_BLOCK + lax.broadcasted_iota(jnp.int32, (1, ROW_BLOCK), 1)
    degree, _ = row_layout(wave_ref[0], row)
    rate = diffusion_ref[...] * (0.1 + degree * (degree + 1.0) / (NTRUNC * (NTRUNC + 1.0)))
    decay = jnp.exp(-rate)
    decay_ref[...] = decay
    gain_ref[...] = mean_decay(rate, decay)


def prepare(first_wave, panel, diffusion):
    rows = ROW_STEPS * ROW_BLOCK
    by_rows = pl.BlockSpec((ROW_BLOCK, HALF), lambda i: (i, 0))
    by_cols = pl.BlockSpec((LEV, ROW_BLOCK), lambda i: (0, i))
    return pl.pallas_call(
        prepare_kernel,
        grid=(ROW_STEPS,),
        in_specs=[
            pl.BlockSpec(memory_space=pltpu.SMEM),
            pl.BlockSpec((8 * ROW_BLOCK, 128), lambda i: (i, 0)),
            pl.BlockSpec((LEV, 1), lambda i: (0, 0)),
        ],
        out_specs=[by_rows, by_rows, by_cols, by_cols],
        out_shape=[
            jax.ShapeDtypeStruct((rows, HALF), jnp.bfloat16),
            jax.ShapeDtypeStruct((rows, HALF), jnp.bfloat16),
            jax.ShapeDtypeStruct((LEV, rows), jnp.float32),
            jax.ShapeDtypeStruct((LEV, rows), jnp.float32),
        ],
        compiler_params=pltpu.CompilerParams(vmem_limit_bytes=VMEM),
        cost_estimate=pl.CostEstimate(flops=20_000_000, bytes_accessed=18_000_000, transcendentals=50_000),
        name="prepare",
    )(first_wave, panel, diffusion)


def legendre_kernel(
    wave_ref,
    received_ref,
    high_hbm,
    low_hbm,
    spectral_ref,
    quad_ref,
    decay_ref,
    gain_ref,
    remap_ref,
    scale_ref,
    new_ref,
    out_ref,
    folded,
    panel_high,
    panel_low,
    spread,
    sems,
):
    first = wave_ref[0]
    loads = []
    for index, start in enumerate(CHUNKS[:-1]):
        rows = pl.ds(start, CHUNKS[index + 1] - start)
        for kind, (source, target) in enumerate(((high_hbm, panel_high), (low_hbm, panel_low))):
            loads.append(
                pltpu.make_async_copy(source.at[rows, :], target.at[rows, :], sems.at[index, kind])
            )
            loads[-1].start()

    def latitudes(group):
        rows = [received_ref[(4 * group + q) * LEV : (4 * group + q + 1) * LEV, :] for q in range(4)]
        return jnp.concatenate(regroup(rows), axis=0)

    for group in range(HALF // 128):
        cols = slice(128 * group, 128 * group + 128)
        north = latitudes(group)
        south = mirrored(latitudes(15 - group))
        weight = quad_ref[:, cols]
        for parity, value in ((0, weight * (north + south)), (1, weight * (north - south))):
            high, low = split(value)
            folded[64 * parity : 64 * parity + 64, cols] = high
            folded[128 + 64 * parity : 192 + 64 * parity, cols] = low

    weight_high, weight_low = split(remap_ref[...])
    weights = jnp.concatenate([weight_high, weight_high, weight_low], axis=1)
    for index, start in enumerate(CHUNKS[:-1]):
        stop = CHUNKS[index + 1]
        rows = slice(start, stop)
        row = start + lax.broadcasted_iota(jnp.int32, (1, stop - start), 1)
        _, combination = row_layout(first, row)
        loads[2 * index].wait()
        loads[2 * index + 1].wait()
        products = mxu(folded[...], panel_high[rows, :], NT) + mxu(folded[...], panel_low[rows, :], NT)
        products = products[:128] + products[128:]
        forcing = products[96:]
        for group in range(3):
            forcing = jnp.where(combination == group, products[32 * group : 32 * group + 32], forcing)
        decay = decay_ref[:, rows]
        gain = gain_ref[:, rows]
        advanced = (
            jnp.concatenate([decay, decay], axis=0) * spectral_ref[:, rows]
            + jnp.concatenate([gain, gain], axis=0) * forcing
        )
        stop = min(stop, ROWS)
        new_ref[:, start:stop] = advanced[:, : stop - start]
        high, low = split(advanced)
        mixed = mxu(weights, jnp.concatenate([high, low, high], axis=0), NN)
        for part, value in enumerate(split(mixed)):
            zero = jnp.zeros_like(value)
            for group in range(4):
                place = slice(128 * part + 32 * group, 128 * part + 32 * group + 32)
                spread[place, rows] = jnp.where(combination == group, value, zero)
    total = mxu(spread[...], panel_high[...], NN) + mxu(spread[...], panel_low[...], NN)
    total = total[:128] + total[128:]

    scale = scale_ref[...]

    def store(group, value):
        parts = regroup([value[LEV * part : LEV * part + LEV] for part in range(4)])
        for q in range(4):
            out_ref[(4 * group + q) * LEV : (4 * group + q + 1) * LEV, :] = parts[q]

    for group in range(HALF // 128):
        cols = slice(128 * group, 128 * group + 128)
        even = total[:64, cols] * scale
        odd = total[64:, cols] * scale
        store(group, even + odd)
        store(15 - group, mirrored(even - odd))


def legendre(first_wave, received, prepared, spectral, quad_weights, remap, scale):
    high, low, decay, gain = prepared
    vmem = pl.BlockSpec(memory_space=pltpu.VMEM)
    anywhere = pl.BlockSpec(memory_space=pl.ANY)
    return pl.pallas_call(
        legendre_kernel,
        in_specs=[pl.BlockSpec(memory_space=pltpu.SMEM), vmem, anywhere, anywhere] + [vmem] * 6,
        out_specs=[vmem, vmem],
        out_shape=[
            jax.ShapeDtypeStruct((2 * LEV, ROWS), jnp.float32),
            jax.ShapeDtypeStruct((4 * PAIRS, 128), jnp.float32),
        ],
        scratch_shapes=[
            pltpu.VMEM((256, HALF), jnp.bfloat16),
            pltpu.VMEM((ROWS_PAD, HALF), jnp.bfloat16),
            pltpu.VMEM((ROWS_PAD, HALF), jnp.bfloat16),
            pltpu.VMEM((256, ROWS_PAD), jnp.bfloat16),
            pltpu.SemaphoreType.DMA((len(CHUNKS) - 1, 2)),
        ],
        compiler_params=pltpu.CompilerParams(vmem_limit_bytes=VMEM),
        name="legendre",
    )(first_wave, received, high, low, spectral, quad_weights, decay, gain, remap, scale)


def inverse_kernel(waves_ref, received_ref, table_hbm, out_hbm, turned, table, grid, load_sems, store_sems):
    count = QUARTER // LON_BLOCK

    def load(parity):
        return pltpu.make_async_copy(table_hbm.at[parity], table.at[parity], load_sems.at[parity])

    def store(index, part):
        begin = (
            index * LON_BLOCK,
            FOLD - (index + 1) * LON_BLOCK,
            FOLD + index * LON_BLOCK,
            NLON - (index + 1) * LON_BLOCK,
        )[part]
        cols = pl.ds(begin, LON_BLOCK)
        return pltpu.make_async_copy(grid.at[:, cols], out_hbm.at[:, cols], store_sems.at[index, part])

    load(0).start()
    load(1).start()
    waves = wave_columns(waves_ref)
    parts = regroup([received_ref[pl.ds(level, PAIRS, stride=4), :] for level in range(4)])
    for parity in range(2):
        half_cos, half_sin = cos_sin(waves[parity])
        real, imag = parts[2 * parity], parts[2 * parity + 1]
        for component, value in (
            (0, real * half_cos + imag * half_sin),
            (1, imag * half_cos - real * half_sin),
        ):
            high, low = split(value.T)
            for copy in range(2):
                cols = slice(PAIRS * copy, PAIRS * copy + PAIRS)
                turned[parity, component, :128, cols] = high
                turned[parity, component, 128:, cols] = low
    for index in range(count):
        cols = slice(index * LON_BLOCK, index * LON_BLOCK + LON_BLOCK)
        near, far = [], []
        for parity in range(2):
            if index == 0:
                load(parity).wait()
            sums = []
            for component in range(2):
                right = table[parity, component, :, :, cols].reshape(2 * PAIRS, LON_BLOCK)
                product = mxu(turned[parity, component], right, NN)
                sums.append(product[:128] + product[128:])
            near.append(sums[0] + sums[1])
            far.append(sums[parity] - sums[1 - parity])
        for part, value in enumerate(
            (
                near[0] + near[1],
                mirrored_wide(far[0] + far[1]),
                near[0] - near[1],
                mirrored_wide(far[0] - far[1]),
            )
        ):
            begin = (
                index * LON_BLOCK,
                FOLD - (index + 1) * LON_BLOCK,
                FOLD + index * LON_BLOCK,
                NLON - (index + 1) * LON_BLOCK,
            )[part]
            grid[:, begin : begin + LON_BLOCK] = value
            store(index, part).start()
    for index in range(count):
        for part in range(4):
            store(index, part).wait()


def inverse(waves, received, table):
    vmem = pl.BlockSpec(memory_space=pltpu.VMEM)
    return pl.pallas_call(
        inverse_kernel,
        in_specs=[vmem, vmem, pl.BlockSpec(memory_space=pl.ANY)],
        out_specs=pl.BlockSpec(memory_space=pl.ANY),
        out_shape=jax.ShapeDtypeStruct((128, NLON), jnp.float32),
        scratch_shapes=[
            pltpu.VMEM((2, 2, 256, 2 * PAIRS), jnp.bfloat16),
            pltpu.VMEM((2, 2, 2, PAIRS, QUARTER), jnp.bfloat16),
            pltpu.VMEM((128, NLON), jnp.float32),
            pltpu.SemaphoreType.DMA((2,)),
            pltpu.SemaphoreType.DMA((QUARTER // LON_BLOCK, 4)),
        ],
        compiler_params=pltpu.CompilerParams(vmem_limit_bytes=VMEM),
        name="inverse",
    )(waves, received, table)


def remap_matrix(bounds):
    lower = bounds[:, :1]
    upper = bounds[:, 1:]
    source = jnp.arange(LEV, dtype=jnp.int32)[None, :]
    crossing = jnp.minimum(upper, (source + 1) * SUBDIV) - jnp.maximum(lower, source * SUBDIV)
    weights = jnp.maximum(crossing, 0).astype(jnp.float32) / (upper - lower).astype(jnp.float32)
    empty = jnp.zeros_like(weights)
    return jnp.block([[weights, empty], [empty, weights]])


def exchange(block):
    moved = lax.all_to_all(block.reshape(PAIRS, 4, 128), ("lat", "lev"), 0, 0, tiled=True)
    return moved.reshape(4 * PAIRS, 128)


def body(tendency, spectral, panel, quad_weights, diffusion, waves, bounds):
    own_pair = lax.axis_index("lat") * lax.axis_size("lev") + lax.axis_index("lev")
    wave_rows = waves.reshape(PAIRS // 128, 128)
    first_wave = lax.dynamic_slice_in_dim(waves, own_pair, 1)
    even_scale = jnp.where(first_wave == 0, 1.0, 2.0).astype(jnp.float32)
    odd_scale = jnp.full((1,), 2.0, jnp.float32)
    scale = jnp.repeat(jnp.concatenate([even_scale, odd_scale]), 2 * LEV)[:, None] / math.sqrt(NLON)

    coeffs, table = forward(wave_rows, tendency.reshape(128, NLON))
    spectral_rows = jnp.pad(spectral.reshape(2 * LEV, ROWS), ((0, 0), (0, ROWS_PAD - ROWS)))
    advanced, returned = legendre(
        first_wave,
        exchange(coeffs),
        prepare(first_wave, panel.reshape(8 * ROWS, 128), diffusion[:, None]),
        spectral_rows,
        quad_weights[None, :],
        remap_matrix(bounds),
        scale,
    )
    grid = inverse(wave_rows, exchange(returned), table)
    return (grid.reshape(tendency.shape), advanced.reshape(spectral.shape))


def solution(mesh):
    return jax.shard_map(
        body,
        mesh=mesh,
        in_specs=(
            P("lev", "lat", None),
            P(("lat", "lev"), None, None, None),
            P(("lat", "lev"), None, None),
            P(),
            P(),
            P(),
            P(),
        ),
        out_specs=(P("lev", "lat", None), P(("lat", "lev"), None, None, None)),
        check_vma=False,
    )
```

```python
import math

import jax
import jax.numpy as jnp
from jax import lax
from jax.experimental import pallas as pl
from jax.experimental.pallas import tpu as pltpu
from jax.sharding import PartitionSpec as P

NTRUNC = 2048
SUBDIV = 8
NLON = 4096
TURN = 2 * NLON
FOLD = NLON // 2
QUARTER = NLON // 4
PAIRS = 256
ROWS = 2049
HALF = 1024
LEV = 16
ROW_BLOCK = 512
ROWS_PAD = 2176
CHUNKS = (0, 1024, ROWS_PAD)
LON_CUTS = (0, 512, 768, 1024)
VMEM = 58 * 1024 * 1024
NT = (((1,), (1,)), ((), ()))
NN = (((1,), (0,)), ((), ()))


def split(value):
    high = value.astype(jnp.bfloat16)
    low = (value - high.astype(jnp.float32)).astype(jnp.bfloat16)
    return (high, low)


def mxu(left, right, dims):
    return lax.dot_general(left, right, dims, preferred_element_type=jnp.float32)


def regroup(parts):
    return [
        jnp.concatenate([part[:, 32 * group : 32 * group + 32] for part in parts], axis=1)
        for group in range(4)
    ]


def cos_sin(turns):
    quadrant = (turns + TURN // 8) >> 11
    angle = (turns - (quadrant << 11)).astype(jnp.float32) * (2.0 * math.pi / TURN)
    sq = angle * angle
    sin = angle * (
        1.0 + sq * (-1.0 / 6 + sq * (1.0 / 120 + sq * (-1.0 / 5040 + sq * (1.0 / 362880))))
    )
    cos = 1.0 + sq * (
        -0.5 + sq * (1.0 / 24 + sq * (-1.0 / 720 + sq * (1.0 / 40320 + sq * (-1.0 / 3628800))))
    )
    swap = (quadrant & 1) == 1
    first = jnp.where(swap, sin, cos)
    second = jnp.where(swap, cos, sin)
    turned = quadrant & 3
    cos_out = jnp.where((turned == 1) | (turned == 2), -first, first)
    sin_out = jnp.where(turned >= 2, -second, second)
    return (cos_out, sin_out)


def mirrored(block):
    lane = lax.broadcasted_iota(jnp.int32, block.shape, 1)
    return jnp.take_along_axis(block, 127 - lane, axis=1)


def mirrored_wide(block):
    width = block.shape[1]
    parts = [mirrored(block[:, start - 128 : start]) for start in range(width, 0, -128)]
    return jnp.concatenate(parts, axis=1)


def wave_columns(waves_ref):
    halves = []
    for half in range(PAIRS // 128):
        row = waves_ref[half : half + 1, :].astype(jnp.float32)
        halves.append(jnp.broadcast_to(row, (128, 128)).T.astype(jnp.int32))
    wave = jnp.concatenate(halves, axis=0)
    even = jnp.where((wave & 1) == 1, NTRUNC - 1 - wave, wave)
    return (even, NTRUNC - 1 - even)


def mean_decay(rate, decay):
    series = jnp.full_like(rate, 1.0 / math.factorial(11))
    for order in range(10, 0, -1):
        series = 1.0 / math.factorial(order) - rate * series
    return jnp.where(rate < 1.0, series, (1.0 - decay) / rate)


def forward_kernel(
    waves_hbm, field_hbm, out_ref, table_hbm, waves_ref, field, folded, table, sems, load_sems
):
    loads = []
    for index in range(4):
        rows = pl.ds(32 * index, 32)
        loads.append(
            pltpu.make_async_copy(field_hbm.at[rows, :], field.at[rows, :], load_sems.at[index])
        )
    load_waves = pltpu.make_async_copy(waves_hbm, waves_ref, sems.at[2])
    load_waves.start()
    for load in loads:
        load.start()
    load_waves.wait()
    waves = wave_columns(waves_ref)
    lane = lax.broadcasted_iota(jnp.int32, (32, 128), 1)
    half_steps = [[], []]

    def build(parity):
        for start in range(0, PAIRS, 32):
            rows = slice(start, start + 32)
            wave = waves[parity][rows]
            half_cos, half_sin = cos_sin(wave)
            half_steps[parity].append((half_cos, half_sin))
            cos, sin = cos_sin((wave * (2 * lane + 1)) & (TURN - 1))
            last_cos = jnp.broadcast_to(cos[:, 127:], cos.shape)
            last_sin = jnp.broadcast_to(sin[:, 127:], sin.shape)
            turn_cos = last_cos * half_cos - last_sin * half_sin
            turn_sin = last_sin * half_cos + last_cos * half_sin
            for block in range(QUARTER // 128):
                cols = slice(block * 128, block * 128 + 128)
                for component, value in ((0, cos), (1, -sin)):
                    high, low = split(value)
                    table[parity, component, 0, rows, cols] = high
                    table[parity, component, 1, rows, cols] = low
                cos, sin = (cos * turn_cos - sin * turn_sin, sin * turn_cos + cos * turn_sin)

    def store(parity):
        return pltpu.make_async_copy(table.at[parity], table_hbm.at[parity], sems.at[parity])

    for parity in range(2):
        build(parity)
        store(parity).start()
    for load in loads:
        load.wait()
    parts = []
    for parity in range(2):
        for start in range(0, QUARTER, 128):
            near = slice(start, start + 128)
            head, tail = field[:, near], field[:, FOLD - 128 - start : FOLD - start]
            east_head = field[:, start + FOLD : start + FOLD + 128]
            east_tail = field[:, NLON - 128 - start : NLON - start]
            if parity == 0:
                head, tail = head + east_head, tail + east_tail
            else:
                head, tail = head - east_head, tail - east_tail
            tail = mirrored(tail)
            for component, value in ((parity, head + tail), (1 - parity, head - tail)):
                high, low = split(value)
                folded[parity, component, :128, near] = high
                folded[parity, component, 128:, near] = low
        sums = []
        for component in range(2):
            left = table[parity, component].reshape(2 * PAIRS, QUARTER)
            product = mxu(left, folded[parity, component], NT)
            product = product[:, :128] + product[:, 128:]
            sums.append((product[:PAIRS] + product[PAIRS:]) * (1.0 / math.sqrt(NLON)))
        half_cos = jnp.concatenate([item[0] for item in half_steps[parity]], axis=0)
        half_sin = jnp.concatenate([item[1] for item in half_steps[parity]], axis=0)
        parts += [sums[0] * half_cos - sums[1] * half_sin, sums[0] * half_sin + sums[1] * half_cos]
    for level, value in enumerate(regroup(parts)):
        out_ref[pl.ds(level, PAIRS, stride=4), :] = value
    for parity in range(2):
        store(parity).wait()


def forward(waves, field):
    return pl.pallas_call(
        forward_kernel,
        in_specs=[pl.BlockSpec(memory_space=pl.ANY)] * 2,
        out_specs=[pl.BlockSpec(memory_space=pltpu.VMEM), pl.BlockSpec(memory_space=pl.ANY)],
        out_shape=[
            jax.ShapeDtypeStruct((4 * PAIRS, 128), jnp.float32),
            jax.ShapeDtypeStruct((2, 2, 2, PAIRS, QUARTER), jnp.bfloat16),
        ],
        scratch_shapes=[
            pltpu.VMEM((PAIRS // 128, 128), jnp.int32),
            pltpu.VMEM((128, NLON), jnp.float32),
            pltpu.VMEM((2, 2, 256, QUARTER), jnp.bfloat16),
            pltpu.VMEM((2, 2, 2, PAIRS, QUARTER), jnp.bfloat16),
            pltpu.SemaphoreType.DMA((3,)),
            pltpu.SemaphoreType.DMA((4,)),
        ],
        compiler_params=pltpu.CompilerParams(vmem_limit_bytes=VMEM),
        name="forward",
    )(waves, field)


def row_layout(first, row):
    leading = row < NTRUNC - first
    degree = jnp.where(leading, first + row, row - 1).astype(jnp.float32)
    parity = jnp.where(leading, row, row + first) & 1
    slot = jnp.where(leading, first & 1, 1 - (first & 1))
    return (degree, 2 * parity + slot)


def own_wave(waves_ref):
    return waves_ref[lax.axis_index("lat") * lax.axis_size("lev") + lax.axis_index("lev")]


def column(values_ref, shape):
    row = lax.broadcasted_iota(jnp.int32, shape, 0) % LEV
    result = jnp.full(shape, values_ref[0])
    for index in range(1, LEV):
        result = jnp.where(row == index, values_ref[index], result)
    return result


def prepare_kernel(waves_ref, diffusion_ref, panel_ref, high_ref, low_ref, decay_ref, gain_ref):
    step = pl.program_id(0)
    last = ROWS // ROW_BLOCK

    def divide(rows, keep):
        for chunk in range(8):
            cols = slice(128 * chunk, 128 * chunk + 128)
            high, low = split(keep(panel_ref[pl.ds(chunk, rows, stride=8), :]))
            high_ref[:rows, cols] = high
            low_ref[:rows, cols] = low
        row = step * ROW_BLOCK + lax.broadcasted_iota(jnp.int32, (1, rows), 1)
        degree, _ = row_layout(own_wave(waves_ref), row)
        scaled = 0.1 + degree * (degree + 1.0) / (NTRUNC * (NTRUNC + 1.0))
        rate = column(diffusion_ref, (LEV, rows)) * scaled
        decay = jnp.exp(-rate)
        decay_ref[:, :rows] = decay
        gain_ref[:, :rows] = mean_decay(rate, decay)

    @pl.when(step < last)
    def _():
        divide(ROW_BLOCK, lambda value: value)

    @pl.when(step == last)
    def _():
        rows = ROWS_PAD - last * ROW_BLOCK
        inside = lax.broadcasted_iota(jnp.int32, (rows, 128), 0) < ROWS - last * ROW_BLOCK
        divide(rows, lambda value: jnp.where(inside, value, 0.0))


def prepare(waves, panel, diffusion):
    by_rows = pl.BlockSpec((ROW_BLOCK, HALF), lambda i: (i, 0))
    by_cols = pl.BlockSpec((LEV, ROW_BLOCK), lambda i: (0, i))
    return pl.pallas_call(
        prepare_kernel,
        grid=(ROWS // ROW_BLOCK + 1,),
        in_specs=[
            pl.BlockSpec(memory_space=pltpu.SMEM),
            pl.BlockSpec(memory_space=pltpu.SMEM),
            pl.BlockSpec((8 * ROW_BLOCK, 128), lambda i: (i, 0)),
        ],
        out_specs=[by_rows, by_rows, by_cols, by_cols],
        out_shape=[
            jax.ShapeDtypeStruct((ROWS_PAD, HALF), jnp.bfloat16),
            jax.ShapeDtypeStruct((ROWS_PAD, HALF), jnp.bfloat16),
            jax.ShapeDtypeStruct((LEV, ROWS_PAD), jnp.float32),
            jax.ShapeDtypeStruct((LEV, ROWS_PAD), jnp.float32),
        ],
        compiler_params=pltpu.CompilerParams(vmem_limit_bytes=VMEM),
        cost_estimate=pl.CostEstimate(flops=20_000_000, bytes_accessed=18_000_000, transcendentals=50_000),
        name="prepare",
    )(waves, diffusion, panel)


def remap_matrix(bounds_ref):
    shape = (2 * LEV, 2 * LEV)
    target = lax.broadcasted_iota(jnp.int32, shape, 0)
    source = lax.broadcasted_iota(jnp.int32, shape, 1)
    lower = column(bounds_ref.at[0], shape)
    upper = column(bounds_ref.at[1], shape)
    level = source % LEV
    crossing = jnp.minimum(upper, (level + 1) * SUBDIV) - jnp.maximum(lower, level * SUBDIV)
    crossing = jnp.where(target // LEV == source // LEV, jnp.maximum(crossing, 0), 0)
    return crossing.astype(jnp.float32) / (upper - lower).astype(jnp.float32)


def legendre_kernel(
    waves_ref,
    bounds_ref,
    received_ref,
    high_hbm,
    low_hbm,
    spectral_hbm,
    quad_hbm,
    decay_hbm,
    gain_hbm,
    new_hbm,
    out_ref,
    folded,
    panel_high,
    panel_low,
    spread,
    spectral_ref,
    quad_ref,
    decay_ref,
    gain_ref,
    tail,
    new_ref,
    sems,
    small_sems,
):
    loads = []
    for index, start in enumerate(CHUNKS[:-1]):
        rows = pl.ds(start, CHUNKS[index + 1] - start)
        for kind, (source, target) in enumerate(((high_hbm, panel_high), (low_hbm, panel_low))):
            loads.append(
                pltpu.make_async_copy(source.at[rows, :], target.at[rows, :], sems.at[index, kind])
            )
    small = [
        pltpu.make_async_copy(source, target, small_sems.at[index])
        for index, (source, target) in enumerate(
            (
                (quad_hbm, quad_ref),
                (spectral_hbm, spectral_ref),
                (decay_hbm, decay_ref),
                (gain_hbm, gain_ref),
            )
        )
    ]
    small[0].start()
    loads[0].start()
    loads[1].start()
    for copy in small[1:] + loads[2:]:
        copy.start()
    first = own_wave(waves_ref)
    tail[...] = jnp.zeros_like(tail)
    weight_high, weight_low = split(remap_matrix(bounds_ref))
    weights = jnp.concatenate([weight_high, weight_high, weight_low], axis=1)
    small[0].wait()

    def latitudes(group):
        rows = [received_ref[(4 * group + q) * LEV : (4 * group + q + 1) * LEV, :] for q in range(4)]
        return jnp.concatenate(regroup(rows), axis=0)

    for group in range(HALF // 128):
        cols = slice(128 * group, 128 * group + 128)
        north = latitudes(group)
        south = mirrored(latitudes(15 - group))
        weight = quad_ref[:, cols]
        for parity, value in ((0, weight * (north + south)), (1, weight * (north - south))):
            high, low = split(value)
            folded[64 * parity : 64 * parity + 64, cols] = high
            folded[128 + 64 * parity : 192 + 64 * parity, cols] = low

    for index, start in enumerate(CHUNKS[:-1]):
        stop = CHUNKS[index + 1]
        rows = slice(start, stop)
        row = start + lax.broadcasted_iota(jnp.int32, (1, stop - start), 1)
        _, combination = row_layout(first, row)
        loads[2 * index].wait()
        loads[2 * index + 1].wait()
        products = mxu(folded[...], panel_high[rows, :], NT) + mxu(folded[...], panel_low[rows, :], NT)
        products = products[:128] + products[128:]
        forcing = products[96:]
        for group in range(3):
            forcing = jnp.where(combination == group, products[32 * group : 32 * group + 32], forcing)
        if index == 0:
            for copy in small[1:]:
                copy.wait()
            tail[:, :1] = spectral_ref[:, ROWS - 1 :]
        decay = decay_ref[:, rows]
        gain = gain_ref[:, rows]
        state = spectral_ref[:, start : min(stop, ROWS - 1)]
        if stop > ROWS:
            state = jnp.concatenate([state, tail[...]], axis=1)
        advanced = (
            jnp.concatenate([decay, decay], axis=0) * state
            + jnp.concatenate([gain, gain], axis=0) * forcing
        )
        stop = min(stop, ROWS)
        new_ref[:, start:stop] = advanced[:, : stop - start]
        high, low = split(advanced)
        mixed = mxu(weights, jnp.concatenate([high, low, high], axis=0), NN)
        for part, value in enumerate(split(mixed)):
            zero = jnp.zeros_like(value)
            for group in range(4):
                place = slice(128 * part + 32 * group, 128 * part + 32 * group + 32)
                spread[place, rows] = jnp.where(combination == group, value, zero)
    store_new = pltpu.make_async_copy(new_ref, new_hbm, small_sems.at[4])
    store_new.start()
    total = mxu(spread[...], panel_high[...], NN)
    total = total[:128] + total[128:] + mxu(spread[:128], panel_low[...], NN)

    slot = lax.broadcasted_iota(jnp.int32, (64, 128), 0) // (2 * LEV)
    scale = jnp.where((slot == 0) & (first == 0), 1.0, 2.0) / math.sqrt(NLON)

    def store(group, value):
        parts = regroup([value[LEV * part : LEV * part + LEV] for part in range(4)])
        for q in range(4):
            out_ref[(4 * group + q) * LEV : (4 * group + q + 1) * LEV, :] = parts[q]

    for group in range(HALF // 128):
        cols = slice(128 * group, 128 * group + 128)
        even = total[:64, cols] * scale
        odd = total[64:, cols] * scale
        store(group, even + odd)
        store(15 - group, mirrored(even - odd))
    store_new.wait()


def legendre(waves, bounds, received, prepared, spectral, quad_weights):
    high, low, decay, gain = prepared
    vmem = pl.BlockSpec(memory_space=pltpu.VMEM)
    smem = pl.BlockSpec(memory_space=pltpu.SMEM)
    anywhere = pl.BlockSpec(memory_space=pl.ANY)
    return pl.pallas_call(
        legendre_kernel,
        in_specs=[smem, smem, vmem] + [anywhere] * 6,
        out_specs=[anywhere, vmem],
        out_shape=[
            jax.ShapeDtypeStruct((2 * LEV, ROWS), jnp.float32),
            jax.ShapeDtypeStruct((4 * PAIRS, 128), jnp.float32),
        ],
        scratch_shapes=[
            pltpu.VMEM((256, HALF), jnp.bfloat16),
            pltpu.VMEM((ROWS_PAD, HALF), jnp.bfloat16),
            pltpu.VMEM((ROWS_PAD, HALF), jnp.bfloat16),
            pltpu.VMEM((256, ROWS_PAD), jnp.bfloat16),
            pltpu.VMEM((2 * LEV, ROWS), jnp.float32),
            pltpu.VMEM((1, HALF), jnp.float32),
            pltpu.VMEM((LEV, ROWS_PAD), jnp.float32),
            pltpu.VMEM((LEV, ROWS_PAD), jnp.float32),
            pltpu.VMEM((2 * LEV, 128), jnp.float32),
            pltpu.VMEM((2 * LEV, ROWS), jnp.float32),
            pltpu.SemaphoreType.DMA((len(CHUNKS) - 1, 2)),
            pltpu.SemaphoreType.DMA((5,)),
        ],
        compiler_params=pltpu.CompilerParams(vmem_limit_bytes=VMEM),
        name="legendre",
    )(waves, bounds, received, high, low, spectral, quad_weights, decay, gain)


def inverse_kernel(
    waves_hbm, received_ref, table_hbm, out_hbm, waves_ref, turned, table, grid, load_sems, store_sems
):
    count = len(LON_CUTS) - 1

    def load(parity):
        return pltpu.make_async_copy(table_hbm.at[parity], table.at[parity], load_sems.at[parity])

    def target(index, part):
        start, stop = LON_CUTS[index], LON_CUTS[index + 1]
        begin = (start, FOLD - stop, FOLD + start, NLON - stop)[part]
        return slice(begin, begin + stop - start)

    def store(index, part):
        cols = target(index, part)
        cols = pl.ds(cols.start, cols.stop - cols.start)
        return pltpu.make_async_copy(grid.at[:, cols], out_hbm.at[:, cols], store_sems.at[index, part])

    load_waves = pltpu.make_async_copy(waves_hbm, waves_ref, load_sems.at[2])
    load_waves.start()
    for parity in range(2):
        load(parity).start()
    parts = regroup([received_ref[pl.ds(level, PAIRS, stride=4), :] for level in range(4)])
    load_waves.wait()
    waves = wave_columns(waves_ref)
    for parity in range(2):
        half_cos, half_sin = cos_sin(waves[parity])
        real, imag = parts[2 * parity], parts[2 * parity + 1]
        for component, value in (
            (0, real * half_cos + imag * half_sin),
            (1, imag * half_cos - real * half_sin),
        ):
            high, low = split(value.T)
            for copy in range(2):
                cols = slice(PAIRS * copy, PAIRS * copy + PAIRS)
                turned[parity, component, :128, cols] = high
                turned[parity, component, 128:, cols] = low
    for index in range(count):
        cols = slice(LON_CUTS[index], LON_CUTS[index + 1])
        near, far = [], []
        for parity in range(2):
            if index == 0:
                load(parity).wait()
            sums = []
            for component in range(2):
                right = table[parity, component, :, :, cols].reshape(2 * PAIRS, cols.stop - cols.start)
                product = mxu(turned[parity, component], right, NN)
                sums.append(product[:128] + product[128:])
            near.append(sums[0] + sums[1])
            far.append(sums[parity] - sums[1 - parity])
        for part, value in enumerate(
            (
                near[0] + near[1],
                mirrored_wide(far[0] + far[1]),
                near[0] - near[1],
                mirrored_wide(far[0] - far[1]),
            )
        ):
            grid[:, target(index, part)] = value
            store(index, part).start()
    for index in range(count):
        for part in range(4):
            store(index, part).wait()


def inverse(waves, received, table):
    vmem = pl.BlockSpec(memory_space=pltpu.VMEM)
    return pl.pallas_call(
        inverse_kernel,
        in_specs=[pl.BlockSpec(memory_space=pl.ANY), vmem, pl.BlockSpec(memory_space=pl.ANY)],
        out_specs=pl.BlockSpec(memory_space=pl.ANY),
        out_shape=jax.ShapeDtypeStruct((128, NLON), jnp.float32),
        scratch_shapes=[
            pltpu.VMEM((PAIRS // 128, 128), jnp.int32),
            pltpu.VMEM((2, 2, 256, 2 * PAIRS), jnp.bfloat16),
            pltpu.VMEM((2, 2, 2, PAIRS, QUARTER), jnp.bfloat16),
            pltpu.VMEM((128, NLON), jnp.float32),
            pltpu.SemaphoreType.DMA((3,)),
            pltpu.SemaphoreType.DMA((len(LON_CUTS) - 1, 4)),
        ],
        compiler_params=pltpu.CompilerParams(vmem_limit_bytes=VMEM),
        name="inverse",
    )(waves, received, table)


def exchange(block):
    moved = lax.all_to_all(block.reshape(PAIRS, 4, 128), ("lat", "lev"), 0, 0, tiled=True)
    return moved.reshape(4 * PAIRS, 128)


def body(tendency, spectral, panel, quad_weights, diffusion, waves, bounds):
    wave_rows = waves.reshape(PAIRS // 128, 128)
    coeffs, table = forward(wave_rows, tendency.reshape(128, NLON))
    advanced, returned = legendre(
        waves,
        bounds.T,
        exchange(coeffs),
        prepare(waves, panel.reshape(8 * ROWS, 128), diffusion),
        spectral.reshape(2 * LEV, ROWS),
        quad_weights[None, :],
    )
    grid = inverse(wave_rows, exchange(returned), table)
    return (grid.reshape(tendency.shape), advanced.reshape(spectral.shape))


def solution(mesh):
    return jax.shard_map(
        body,
        mesh=mesh,
        in_specs=(
            P("lev", "lat", None),
            P(("lat", "lev"), None, None, None),
            P(("lat", "lev"), None, None),
            P(),
            P(),
            P(),
            P(),
        ),
        out_specs=(P("lev", "lat", None), P(("lat", "lev"), None, None, None)),
        check_vma=False,
    )
```

```python
import math

import jax
import jax.numpy as jnp
from jax import lax
from jax.experimental import pallas as pl
from jax.experimental.pallas import tpu as pltpu
from jax.sharding import PartitionSpec as P

NTRUNC = 2048
SUBDIV = 8
NLON = 4096
TURN = 2 * NLON
FOLD = NLON // 2
QUARTER = NLON // 4
PAIRS = 256
ROWS = 2049
HALF = 1024
LEV = 16
ROW_BLOCK = 512
ROWS_PAD = 2176
CHUNKS = (0, 1024, ROWS_PAD)
LON_CUTS = (0, 512, 768, 1024)
VMEM = 58 * 1024 * 1024
VMEM_LEGENDRE = 52 * 1024 * 1024
VMEM_INVERSE = 48 * 1024 * 1024
NT = (((1,), (1,)), ((), ()))
NN = (((1,), (0,)), ((), ()))


def split(value):
    high = value.astype(jnp.bfloat16)
    low = (value - high.astype(jnp.float32)).astype(jnp.bfloat16)
    return (high, low)


def mxu(left, right, dims):
    return lax.dot_general(left, right, dims, preferred_element_type=jnp.float32)


def regroup(parts):
    return [
        jnp.concatenate([part[:, 32 * group : 32 * group + 32] for part in parts], axis=1)
        for group in range(4)
    ]


def cos_sin(turns):
    quadrant = (turns + TURN // 8) >> 11
    angle = (turns - (quadrant << 11)).astype(jnp.float32) * (2.0 * math.pi / TURN)
    sq = angle * angle
    sin = angle * (
        1.0 + sq * (-1.0 / 6 + sq * (1.0 / 120 + sq * (-1.0 / 5040 + sq * (1.0 / 362880))))
    )
    cos = 1.0 + sq * (
        -0.5 + sq * (1.0 / 24 + sq * (-1.0 / 720 + sq * (1.0 / 40320 + sq * (-1.0 / 3628800))))
    )
    swap = (quadrant & 1) == 1
    first = jnp.where(swap, sin, cos)
    second = jnp.where(swap, cos, sin)
    turned = quadrant & 3
    cos_out = jnp.where((turned == 1) | (turned == 2), -first, first)
    sin_out = jnp.where(turned >= 2, -second, second)
    return (cos_out, sin_out)


def mirrored(block):
    lane = lax.broadcasted_iota(jnp.int32, block.shape, 1)
    return jnp.take_along_axis(block, 127 - lane, axis=1)


def mirrored_wide(block):
    width = block.shape[1]
    parts = [mirrored(block[:, start - 128 : start]) for start in range(width, 0, -128)]
    return jnp.concatenate(parts, axis=1)


def wave_columns(waves_ref):
    halves = []
    for half in range(PAIRS // 128):
        row = waves_ref[half : half + 1, :].astype(jnp.float32)
        halves.append(jnp.broadcast_to(row, (128, 128)).T.astype(jnp.int32))
    wave = jnp.concatenate(halves, axis=0)
    even = jnp.where((wave & 1) == 1, NTRUNC - 1 - wave, wave)
    return (even, NTRUNC - 1 - even)


def mean_decay(rate, decay):
    series = jnp.full_like(rate, 1.0 / math.factorial(11))
    for order in range(10, 0, -1):
        series = 1.0 / math.factorial(order) - rate * series
    return jnp.where(rate < 1.0, series, (1.0 - decay) / rate)


def forward_kernel(
    waves_hbm, field_hbm, out_ref, table_hbm, waves_ref, field, folded, table, sems
):
    load = pltpu.make_async_copy(field_hbm, field, sems.at[3])
    load_waves = pltpu.make_async_copy(waves_hbm, waves_ref, sems.at[2])
    load_waves.start()
    load.start()
    load_waves.wait()
    waves = wave_columns(waves_ref)
    lane = lax.broadcasted_iota(jnp.int32, (32, 128), 1)
    half_steps = [[], []]

    def build(parity):
        for start in range(0, PAIRS, 32):
            rows = slice(start, start + 32)
            wave = waves[parity][rows]
            half_cos, half_sin = cos_sin(wave)
            half_steps[parity].append((half_cos, half_sin))
            cos, sin = cos_sin((wave * (2 * lane + 1)) & (TURN - 1))
            last_cos = jnp.broadcast_to(cos[:, 127:], cos.shape)
            last_sin = jnp.broadcast_to(sin[:, 127:], sin.shape)
            turn_cos = last_cos * half_cos - last_sin * half_sin
            turn_sin = last_sin * half_cos + last_cos * half_sin
            for block in range(QUARTER // 128):
                cols = slice(block * 128, block * 128 + 128)
                for component, value in ((0, cos), (1, -sin)):
                    high, low = split(value)
                    table[parity, component, 0, rows, cols] = high
                    table[parity, component, 1, rows, cols] = low
                cos, sin = (cos * turn_cos - sin * turn_sin, sin * turn_cos + cos * turn_sin)

    def store(parity):
        return pltpu.make_async_copy(table.at[parity], table_hbm.at[parity], sems.at[parity])

    for parity in range(2):
        build(parity)
        store(parity).start()
    load.wait()
    parts = []
    for parity in range(2):
        for start in range(0, QUARTER, 128):
            near = slice(start, start + 128)
            head, tail = field[:, near], field[:, FOLD - 128 - start : FOLD - start]
            east_head = field[:, start + FOLD : start + FOLD + 128]
            east_tail = field[:, NLON - 128 - start : NLON - start]
            if parity == 0:
                head, tail = head + east_head, tail + east_tail
            else:
                head, tail = head - east_head, tail - east_tail
            tail = mirrored(tail)
            for component, value in ((parity, head + tail), (1 - parity, head - tail)):
                high, low = split(value)
                folded[parity, component, :128, near] = high
                folded[parity, component, 128:, near] = low
        sums = []
        for component in range(2):
            left = table[parity, component].reshape(2 * PAIRS, QUARTER)
            product = mxu(left, folded[parity, component], NT)
            product = product[:, :128] + product[:, 128:]
            sums.append((product[:PAIRS] + product[PAIRS:]) * (1.0 / math.sqrt(NLON)))
        half_cos = jnp.concatenate([item[0] for item in half_steps[parity]], axis=0)
        half_sin = jnp.concatenate([item[1] for item in half_steps[parity]], axis=0)
        parts += [sums[0] * half_cos - sums[1] * half_sin, sums[0] * half_sin + sums[1] * half_cos]
    for level, value in enumerate(regroup(parts)):
        out_ref[pl.ds(level, PAIRS, stride=4), :] = value
    for parity in range(2):
        store(parity).wait()


def forward(waves, field):
    return pl.pallas_call(
        forward_kernel,
        in_specs=[pl.BlockSpec(memory_space=pl.ANY)] * 2,
        out_specs=[pl.BlockSpec(memory_space=pltpu.VMEM), pl.BlockSpec(memory_space=pl.ANY)],
        out_shape=[
            jax.ShapeDtypeStruct((4 * PAIRS, 128), jnp.float32),
            jax.ShapeDtypeStruct((2, 2, 2, PAIRS, QUARTER), jnp.bfloat16),
        ],
        scratch_shapes=[
            pltpu.VMEM((PAIRS // 128, 128), jnp.int32),
            pltpu.VMEM((128, NLON), jnp.float32),
            pltpu.VMEM((2, 2, 256, QUARTER), jnp.bfloat16),
            pltpu.VMEM((2, 2, 2, PAIRS, QUARTER), jnp.bfloat16),
            pltpu.SemaphoreType.DMA((4,)),
        ],
        compiler_params=pltpu.CompilerParams(vmem_limit_bytes=VMEM),
        name="forward",
    )(waves, field)


def row_layout(first, row):
    leading = row < NTRUNC - first
    degree = jnp.where(leading, first + row, row - 1).astype(jnp.float32)
    parity = jnp.where(leading, row, row + first) & 1
    slot = jnp.where(leading, first & 1, 1 - (first & 1))
    return (degree, 2 * parity + slot)


def own_wave(waves_ref):
    return waves_ref[lax.axis_index("lat") * lax.axis_size("lev") + lax.axis_index("lev")]


def column(values_ref, shape):
    row = lax.broadcasted_iota(jnp.int32, shape, 0) % LEV
    result = jnp.full(shape, values_ref[0])
    for index in range(1, LEV):
        result = jnp.where(row == index, values_ref[index], result)
    return result


def prepare_kernel(panel_ref, high_ref, low_ref):
    step = pl.program_id(0)
    last = ROWS // ROW_BLOCK

    def divide(rows, keep):
        for chunk in range(8):
            cols = slice(128 * chunk, 128 * chunk + 128)
            high, low = split(keep(panel_ref[pl.ds(chunk, rows, stride=8), :]))
            high_ref[:rows, cols] = high
            low_ref[:rows, cols] = low

    @pl.when(step < last)
    def _():
        divide(ROW_BLOCK, lambda value: value)

    @pl.when(step == last)
    def _():
        rows = ROWS_PAD - last * ROW_BLOCK
        inside = lax.broadcasted_iota(jnp.int32, (rows, 128), 0) < ROWS - last * ROW_BLOCK
        divide(rows, lambda value: jnp.where(inside, value, 0.0))


def prepare(panel):
    by_rows = pl.BlockSpec((ROW_BLOCK, HALF), lambda i: (i, 0))
    return pl.pallas_call(
        prepare_kernel,
        grid=(ROWS // ROW_BLOCK + 1,),
        in_specs=[pl.BlockSpec((8 * ROW_BLOCK, 128), lambda i: (i, 0))],
        out_specs=[by_rows, by_rows],
        out_shape=[
            jax.ShapeDtypeStruct((ROWS_PAD, HALF), jnp.bfloat16),
            jax.ShapeDtypeStruct((ROWS_PAD, HALF), jnp.bfloat16),
        ],
        compiler_params=pltpu.CompilerParams(vmem_limit_bytes=VMEM),
        cost_estimate=pl.CostEstimate(flops=20_000_000, bytes_accessed=18_000_000, transcendentals=0),
        name="prepare",
    )(panel)


def remap_matrix(bounds_ref):
    shape = (2 * LEV, 2 * LEV)
    target = lax.broadcasted_iota(jnp.int32, shape, 0)
    source = lax.broadcasted_iota(jnp.int32, shape, 1)
    lower = column(bounds_ref.at[0], shape)
    upper = column(bounds_ref.at[1], shape)
    level = source % LEV
    crossing = jnp.minimum(upper, (level + 1) * SUBDIV) - jnp.maximum(lower, level * SUBDIV)
    crossing = jnp.where(target // LEV == source // LEV, jnp.maximum(crossing, 0), 0)
    return crossing.astype(jnp.float32) / (upper - lower).astype(jnp.float32)


def legendre_kernel(
    waves_ref,
    bounds_ref,
    diffusion_ref,
    received_ref,
    high_hbm,
    low_hbm,
    spectral_hbm,
    quad_hbm,
    new_hbm,
    out_ref,
    folded,
    panel_high,
    panel_low,
    spread,
    spectral_ref,
    quad_ref,
    decay_ref,
    gain_ref,
    tail,
    new_ref,
    sems,
    small_sems,
):
    loads = []
    for index, start in enumerate(CHUNKS[:-1]):
        rows = pl.ds(start, CHUNKS[index + 1] - start)
        for kind, (source, target) in enumerate(((high_hbm, panel_high), (low_hbm, panel_low))):
            loads.append(
                pltpu.make_async_copy(source.at[rows, :], target.at[rows, :], sems.at[index, kind])
            )
    small = [
        pltpu.make_async_copy(source, target, small_sems.at[index])
        for index, (source, target) in enumerate(
            (
                (quad_hbm, quad_ref),
                (spectral_hbm, spectral_ref),
            )
        )
    ]
    small[0].start()
    loads[0].start()
    loads[1].start()
    for copy in small[1:] + loads[2:]:
        copy.start()
    first = own_wave(waves_ref)
    tail[...] = jnp.zeros_like(tail)
    weight_high, weight_low = split(remap_matrix(bounds_ref))
    weights = jnp.concatenate([weight_high, weight_high, weight_low], axis=1)
    degree, _ = row_layout(first, lax.broadcasted_iota(jnp.int32, (1, ROWS_PAD), 1))
    strength = column(diffusion_ref, (LEV, 128))
    for start in range(0, ROWS_PAD, 128):
        rows = slice(start, start + 128)
        scaled = 0.1 + degree[:, rows] * (degree[:, rows] + 1.0) / (NTRUNC * (NTRUNC + 1.0))
        rate = strength * scaled
        decay = jnp.exp(-rate)
        decay_ref[:, rows] = decay
        gain_ref[:, rows] = mean_decay(rate, decay)
    small[0].wait()

    def latitudes(group):
        rows = [received_ref[(4 * group + q) * LEV : (4 * group + q + 1) * LEV, :] for q in range(4)]
        return jnp.concatenate(regroup(rows), axis=0)

    for group in range(HALF // 128):
        cols = slice(128 * group, 128 * group + 128)
        north = latitudes(group)
        south = mirrored(latitudes(15 - group))
        weight = quad_ref[:, cols]
        for parity, value in ((0, weight * (north + south)), (1, weight * (north - south))):
            high, low = split(value)
            folded[64 * parity : 64 * parity + 64, cols] = high
            folded[128 + 64 * parity : 192 + 64 * parity, cols] = low

    for index, start in enumerate(CHUNKS[:-1]):
        stop = CHUNKS[index + 1]
        rows = slice(start, stop)
        row = start + lax.broadcasted_iota(jnp.int32, (1, stop - start), 1)
        _, combination = row_layout(first, row)
        loads[2 * index].wait()
        loads[2 * index + 1].wait()
        products = mxu(folded[...], panel_high[rows, :], NT) + mxu(folded[...], panel_low[rows, :], NT)
        products = products[:128] + products[128:]
        forcing = products[96:]
        for group in range(3):
            forcing = jnp.where(combination == group, products[32 * group : 32 * group + 32], forcing)
        if index == 0:
            for copy in small[1:]:
                copy.wait()
            tail[:, :1] = spectral_ref[:, ROWS - 1 :]
        decay = decay_ref[:, rows]
        gain = gain_ref[:, rows]
        state = spectral_ref[:, start : min(stop, ROWS - 1)]
        if stop > ROWS:
            state = jnp.concatenate([state, tail[...]], axis=1)
        advanced = (
            jnp.concatenate([decay, decay], axis=0) * state
            + jnp.concatenate([gain, gain], axis=0) * forcing
        )
        stop = min(stop, ROWS)
        new_ref[:, start:stop] = advanced[:, : stop - start]
        high, low = split(advanced)
        mixed = mxu(weights, jnp.concatenate([high, low, high], axis=0), NN)
        for part, value in enumerate(split(mixed)):
            zero = jnp.zeros_like(value)
            for group in range(4):
                place = slice(128 * part + 32 * group, 128 * part + 32 * group + 32)
                spread[place, rows] = jnp.where(combination == group, value, zero)
    store_new = pltpu.make_async_copy(new_ref, new_hbm, small_sems.at[2])
    store_new.start()
    total = mxu(spread[...], panel_high[...], NN)
    total = total[:128] + total[128:] + mxu(spread[:128], panel_low[...], NN)

    slot = lax.broadcasted_iota(jnp.int32, (64, 128), 0) // (2 * LEV)
    scale = jnp.where((slot == 0) & (first == 0), 1.0, 2.0) / math.sqrt(NLON)

    def store(group, value):
        parts = regroup([value[LEV * part : LEV * part + LEV] for part in range(4)])
        for q in range(4):
            out_ref[(4 * group + q) * LEV : (4 * group + q + 1) * LEV, :] = parts[q]

    for group in range(HALF // 128):
        cols = slice(128 * group, 128 * group + 128)
        even = total[:64, cols] * scale
        odd = total[64:, cols] * scale
        store(group, even + odd)
        store(15 - group, mirrored(even - odd))
    store_new.wait()


def legendre(waves, bounds, diffusion, received, prepared, spectral, quad_weights):
    high, low = prepared
    vmem = pl.BlockSpec(memory_space=pltpu.VMEM)
    smem = pl.BlockSpec(memory_space=pltpu.SMEM)
    anywhere = pl.BlockSpec(memory_space=pl.ANY)
    return pl.pallas_call(
        legendre_kernel,
        in_specs=[smem, smem, smem, vmem] + [anywhere] * 4,
        out_specs=[anywhere, vmem],
        out_shape=[
            jax.ShapeDtypeStruct((2 * LEV, ROWS), jnp.float32),
            jax.ShapeDtypeStruct((4 * PAIRS, 128), jnp.float32),
        ],
        scratch_shapes=[
            pltpu.VMEM((256, HALF), jnp.bfloat16),
            pltpu.VMEM((ROWS_PAD, HALF), jnp.bfloat16),
            pltpu.VMEM((ROWS_PAD, HALF), jnp.bfloat16),
            pltpu.VMEM((256, ROWS_PAD), jnp.bfloat16),
            pltpu.VMEM((2 * LEV, ROWS), jnp.float32),
            pltpu.VMEM((1, HALF), jnp.float32),
            pltpu.VMEM((LEV, ROWS_PAD), jnp.float32),
            pltpu.VMEM((LEV, ROWS_PAD), jnp.float32),
            pltpu.VMEM((2 * LEV, 128), jnp.float32),
            pltpu.VMEM((2 * LEV, ROWS), jnp.float32),
            pltpu.SemaphoreType.DMA((len(CHUNKS) - 1, 2)),
            pltpu.SemaphoreType.DMA((3,)),
        ],
        compiler_params=pltpu.CompilerParams(vmem_limit_bytes=VMEM_LEGENDRE),
        name="legendre",
    )(waves, bounds, diffusion, received, high, low, spectral, quad_weights)


def inverse_kernel(
    waves_hbm, received_ref, table, out_hbm, waves_ref, turned, grid, load_sems, store_sems
):
    count = len(LON_CUTS) - 1

    def target(index, part):
        start, stop = LON_CUTS[index], LON_CUTS[index + 1]
        begin = (start, FOLD - stop, FOLD + start, NLON - stop)[part]
        return slice(begin, begin + stop - start)

    def store(index, part):
        cols = target(index, part)
        cols = pl.ds(cols.start, cols.stop - cols.start)
        return pltpu.make_async_copy(grid.at[:, cols], out_hbm.at[:, cols], store_sems.at[index, part])

    load_waves = pltpu.make_async_copy(waves_hbm, waves_ref, load_sems.at[2])
    load_waves.start()
    parts = regroup([received_ref[pl.ds(level, PAIRS, stride=4), :] for level in range(4)])
    load_waves.wait()
    waves = wave_columns(waves_ref)
    for parity in range(2):
        half_cos, half_sin = cos_sin(waves[parity])
        real, imag = parts[2 * parity], parts[2 * parity + 1]
        for component, value in (
            (0, real * half_cos + imag * half_sin),
            (1, imag * half_cos - real * half_sin),
        ):
            high, low = split(value.T)
            for copy in range(2):
                cols = slice(PAIRS * copy, PAIRS * copy + PAIRS)
                turned[parity, component, :128, cols] = high
                turned[parity, component, 128:, cols] = low
    for index in range(count):
        cols = slice(LON_CUTS[index], LON_CUTS[index + 1])
        near, far = [], []
        for parity in range(2):
            sums = []
            for component in range(2):
                right = table[parity, component, :, :, cols].reshape(2 * PAIRS, cols.stop - cols.start)
                product = mxu(turned[parity, component], right, NN)
                sums.append(product[:128] + product[128:])
            near.append(sums[0] + sums[1])
            far.append(sums[parity] - sums[1 - parity])
        for part, value in enumerate(
            (
                near[0] + near[1],
                mirrored_wide(far[0] + far[1]),
                near[0] - near[1],
                mirrored_wide(far[0] - far[1]),
            )
        ):
            grid[:, target(index, part)] = value
            store(index, part).start()
    for index in range(count):
        for part in range(4):
            store(index, part).wait()


def inverse(waves, received, table):
    vmem = pl.BlockSpec(memory_space=pltpu.VMEM)
    return pl.pallas_call(
        inverse_kernel,
        in_specs=[pl.BlockSpec(memory_space=pl.ANY), vmem, vmem],
        out_specs=pl.BlockSpec(memory_space=pl.ANY),
        out_shape=jax.ShapeDtypeStruct((128, NLON), jnp.float32),
        scratch_shapes=[
            pltpu.VMEM((PAIRS // 128, 128), jnp.int32),
            pltpu.VMEM((2, 2, 256, 2 * PAIRS), jnp.bfloat16),
            pltpu.VMEM((128, NLON), jnp.float32),
            pltpu.SemaphoreType.DMA((3,)),
            pltpu.SemaphoreType.DMA((len(LON_CUTS) - 1, 4)),
        ],
        compiler_params=pltpu.CompilerParams(vmem_limit_bytes=VMEM_INVERSE),
        name="inverse",
    )(waves, received, table)


def exchange(block):
    moved = lax.all_to_all(block.reshape(PAIRS, 4, 128), ("lat", "lev"), 0, 0, tiled=True)
    return moved.reshape(4 * PAIRS, 128)


def body(tendency, spectral, panel, quad_weights, diffusion, waves, bounds):
    wave_rows = waves.reshape(PAIRS // 128, 128)
    coeffs, table = forward(wave_rows, tendency.reshape(128, NLON))
    advanced, returned = legendre(
        waves,
        bounds.T,
        diffusion,
        exchange(coeffs),
        prepare(panel.reshape(8 * ROWS, 128)),
        spectral.reshape(2 * LEV, ROWS),
        quad_weights[None, :],
    )
    grid = inverse(wave_rows, exchange(returned), table)
    return (grid.reshape(tendency.shape), advanced.reshape(spectral.shape))


def solution(mesh):
    return jax.shard_map(
        body,
        mesh=mesh,
        in_specs=(
            P("lev", "lat", None),
            P(("lat", "lev"), None, None, None),
            P(("lat", "lev"), None, None),
            P(),
            P(),
            P(),
            P(),
        ),
        out_specs=(P("lev", "lat", None), P(("lat", "lev"), None, None, None)),
        check_vma=False,
    )
```

```python
import math

import jax
import jax.numpy as jnp
from jax import lax
from jax.experimental import pallas as pl
from jax.experimental.pallas import tpu as pltpu
from jax.sharding import PartitionSpec as P

NTRUNC = 2048
SUBDIV = 8
NLON = 4096
TURN = 2 * NLON
FOLD = NLON // 2
QUARTER = NLON // 4
PAIRS = 256
ROWS = 2049
HALF = 1024
LEV = 16
ROW_BLOCK = 512
ROWS_PAD = 2176
CHUNKS = (0, 896, ROWS_PAD)
LON_CUTS = (0, 512, 768, 1024)
VMEM = 58 * 1024 * 1024
VMEM_LEGENDRE = 52 * 1024 * 1024
VMEM_INVERSE = 48 * 1024 * 1024
NT = (((1,), (1,)), ((), ()))
NN = (((1,), (0,)), ((), ()))


def split(value):
    high = value.astype(jnp.bfloat16)
    low = (value - high.astype(jnp.float32)).astype(jnp.bfloat16)
    return (high, low)


def mxu(left, right, dims):
    return lax.dot_general(left, right, dims, preferred_element_type=jnp.float32)


def regroup(parts):
    return [
        jnp.concatenate([part[:, 32 * group : 32 * group + 32] for part in parts], axis=1)
        for group in range(4)
    ]


def cos_sin(turns):
    quadrant = (turns + TURN // 8) >> 11
    angle = (turns - (quadrant << 11)).astype(jnp.float32) * (2.0 * math.pi / TURN)
    sq = angle * angle
    sin = angle * (
        1.0 + sq * (-1.0 / 6 + sq * (1.0 / 120 + sq * (-1.0 / 5040 + sq * (1.0 / 362880))))
    )
    cos = 1.0 + sq * (
        -0.5 + sq * (1.0 / 24 + sq * (-1.0 / 720 + sq * (1.0 / 40320 + sq * (-1.0 / 3628800))))
    )
    swap = (quadrant & 1) == 1
    first = jnp.where(swap, sin, cos)
    second = jnp.where(swap, cos, sin)
    turned = quadrant & 3
    cos_out = jnp.where((turned == 1) | (turned == 2), -first, first)
    sin_out = jnp.where(turned >= 2, -second, second)
    return (cos_out, sin_out)


def mirrored(block):
    lane = lax.broadcasted_iota(jnp.int32, block.shape, 1)
    return jnp.take_along_axis(block, 127 - lane, axis=1)


def mirrored_wide(block):
    width = block.shape[1]
    parts = [mirrored(block[:, start - 128 : start]) for start in range(width, 0, -128)]
    return jnp.concatenate(parts, axis=1)


def wave_columns(waves_ref):
    halves = []
    for half in range(PAIRS // 128):
        row = waves_ref[half : half + 1, :].astype(jnp.float32)
        halves.append(jnp.broadcast_to(row, (128, 128)).T.astype(jnp.int32))
    wave = jnp.concatenate(halves, axis=0)
    even = jnp.where((wave & 1) == 1, NTRUNC - 1 - wave, wave)
    return (even, NTRUNC - 1 - even)


def mean_decay(rate, decay):
    series = jnp.full_like(rate, 1.0 / math.factorial(11))
    for order in range(10, 0, -1):
        series = 1.0 / math.factorial(order) - rate * series
    return jnp.where(rate < 1.0, series, (1.0 - decay) / rate)


def forward_kernel(
    waves_hbm, field_hbm, out_ref, table_hbm, waves_ref, field, folded, table, sems
):
    load = pltpu.make_async_copy(field_hbm, field, sems.at[3])
    load_waves = pltpu.make_async_copy(waves_hbm, waves_ref, sems.at[2])
    load_waves.start()
    load.start()
    load_waves.wait()
    waves = wave_columns(waves_ref)
    lane = lax.broadcasted_iota(jnp.int32, (32, 128), 1)
    half_steps = [[], []]

    def build(parity):
        for start in range(0, PAIRS, 32):
            rows = slice(start, start + 32)
            wave = waves[parity][rows]
            half_cos, half_sin = cos_sin(wave)
            half_steps[parity].append((half_cos, half_sin))
            cos, sin = cos_sin((wave * (2 * lane + 1)) & (TURN - 1))
            last_cos = jnp.broadcast_to(cos[:, 127:], cos.shape)
            last_sin = jnp.broadcast_to(sin[:, 127:], sin.shape)
            turn_cos = last_cos * half_cos - last_sin * half_sin
            turn_sin = last_sin * half_cos + last_cos * half_sin
            for block in range(QUARTER // 128):
                cols = slice(block * 128, block * 128 + 128)
                for component, value in ((0, cos), (1, -sin)):
                    high, low = split(value)
                    table[parity, component, 0, rows, cols] = high
                    table[parity, component, 1, rows, cols] = low
                cos, sin = (cos * turn_cos - sin * turn_sin, sin * turn_cos + cos * turn_sin)

    def store(parity):
        return pltpu.make_async_copy(table.at[parity], table_hbm.at[parity], sems.at[parity])

    for parity in range(2):
        build(parity)
        store(parity).start()
    load.wait()
    parts = []
    for parity in range(2):
        for start in range(0, QUARTER, 128):
            near = slice(start, start + 128)
            head, tail = field[:, near], field[:, FOLD - 128 - start : FOLD - start]
            east_head = field[:, start + FOLD : start + FOLD + 128]
            east_tail = field[:, NLON - 128 - start : NLON - start]
            if parity == 0:
                head, tail = head + east_head, tail + east_tail
            else:
                head, tail = head - east_head, tail - east_tail
            tail = mirrored(tail)
            for component, value in ((parity, head + tail), (1 - parity, head - tail)):
                high, low = split(value)
                folded[parity, component, :128, near] = high
                folded[parity, component, 128:, near] = low
        sums = []
        for component in range(2):
            left = table[parity, component].reshape(2 * PAIRS, QUARTER)
            product = mxu(left, folded[parity, component], NT)
            product = product[:, :128] + product[:, 128:]
            sums.append((product[:PAIRS] + product[PAIRS:]) * (1.0 / math.sqrt(NLON)))
        half_cos = jnp.concatenate([item[0] for item in half_steps[parity]], axis=0)
        half_sin = jnp.concatenate([item[1] for item in half_steps[parity]], axis=0)
        parts += [sums[0] * half_cos - sums[1] * half_sin, sums[0] * half_sin + sums[1] * half_cos]
    for level, value in enumerate(regroup(parts)):
        out_ref[pl.ds(level, PAIRS, stride=4), :] = value
    for parity in range(2):
        store(parity).wait()


def forward(waves, field):
    return pl.pallas_call(
        forward_kernel,
        in_specs=[pl.BlockSpec(memory_space=pl.ANY)] * 2,
        out_specs=[pl.BlockSpec(memory_space=pltpu.VMEM), pl.BlockSpec(memory_space=pl.ANY)],
        out_shape=[
            jax.ShapeDtypeStruct((4 * PAIRS, 128), jnp.float32),
            jax.ShapeDtypeStruct((2, 2, 2, PAIRS, QUARTER), jnp.bfloat16),
        ],
        scratch_shapes=[
            pltpu.VMEM((PAIRS // 128, 128), jnp.int32),
            pltpu.VMEM((128, NLON), jnp.float32),
            pltpu.VMEM((2, 2, 256, QUARTER), jnp.bfloat16),
            pltpu.VMEM((2, 2, 2, PAIRS, QUARTER), jnp.bfloat16),
            pltpu.SemaphoreType.DMA((4,)),
        ],
        compiler_params=pltpu.CompilerParams(vmem_limit_bytes=VMEM),
        name="forward",
    )(waves, field)


def row_layout(first, row):
    leading = row < NTRUNC - first
    degree = jnp.where(leading, first + row, row - 1).astype(jnp.float32)
    parity = jnp.where(leading, row, row + first) & 1
    slot = jnp.where(leading, first & 1, 1 - (first & 1))
    return (degree, 2 * parity + slot)


def own_wave(waves_ref):
    return waves_ref[lax.axis_index("lat") * lax.axis_size("lev") + lax.axis_index("lev")]


def column(values_ref, shape):
    row = lax.broadcasted_iota(jnp.int32, shape, 0) % LEV
    result = jnp.full(shape, values_ref[0])
    for index in range(1, LEV):
        result = jnp.where(row == index, values_ref[index], result)
    return result


def prepare_kernel(panel_ref, high_ref, low_ref):
    step = pl.program_id(0)
    last = ROWS // ROW_BLOCK

    def divide(rows, keep):
        for chunk in range(8):
            cols = slice(128 * chunk, 128 * chunk + 128)
            high, low = split(keep(panel_ref[pl.ds(chunk, rows, stride=8), :]))
            high_ref[:rows, cols] = high
            low_ref[:rows, cols] = low

    @pl.when(step < last)
    def _():
        divide(ROW_BLOCK, lambda value: value)

    @pl.when(step == last)
    def _():
        rows = ROWS_PAD - last * ROW_BLOCK
        inside = lax.broadcasted_iota(jnp.int32, (rows, 128), 0) < ROWS - last * ROW_BLOCK
        divide(rows, lambda value: jnp.where(inside, value, 0.0))


def prepare(panel):
    by_rows = pl.BlockSpec((ROW_BLOCK, HALF), lambda i: (i, 0))
    return pl.pallas_call(
        prepare_kernel,
        grid=(ROWS // ROW_BLOCK + 1,),
        in_specs=[pl.BlockSpec((8 * ROW_BLOCK, 128), lambda i: (i, 0))],
        out_specs=[by_rows, by_rows],
        out_shape=[
            jax.ShapeDtypeStruct((ROWS_PAD, HALF), jnp.bfloat16),
            jax.ShapeDtypeStruct((ROWS_PAD, HALF), jnp.bfloat16),
        ],
        compiler_params=pltpu.CompilerParams(vmem_limit_bytes=VMEM),
        cost_estimate=pl.CostEstimate(flops=20_000_000, bytes_accessed=18_000_000, transcendentals=0),
        name="prepare",
    )(panel)


def remap_matrix(bounds_ref):
    shape = (2 * LEV, 2 * LEV)
    target = lax.broadcasted_iota(jnp.int32, shape, 0)
    source = lax.broadcasted_iota(jnp.int32, shape, 1)
    lower = column(bounds_ref.at[0], shape)
    upper = column(bounds_ref.at[1], shape)
    level = source % LEV
    crossing = jnp.minimum(upper, (level + 1) * SUBDIV) - jnp.maximum(lower, level * SUBDIV)
    crossing = jnp.where(target // LEV == source // LEV, jnp.maximum(crossing, 0), 0)
    return crossing.astype(jnp.float32) / (upper - lower).astype(jnp.float32)


def legendre_kernel(
    waves_ref,
    bounds_ref,
    diffusion_ref,
    received_ref,
    high_hbm,
    low_hbm,
    spectral_hbm,
    quad_hbm,
    new_hbm,
    out_ref,
    folded,
    panel_high,
    panel_low,
    spread,
    spectral_ref,
    quad_ref,
    decay_ref,
    gain_ref,
    tail,
    new_ref,
    sems,
    small_sems,
):
    loads = []
    for index, start in enumerate(CHUNKS[:-1]):
        rows = pl.ds(start, CHUNKS[index + 1] - start)
        for kind, (source, target) in enumerate(((high_hbm, panel_high), (low_hbm, panel_low))):
            loads.append(
                pltpu.make_async_copy(source.at[rows, :], target.at[rows, :], sems.at[index, kind])
            )
    small = [
        pltpu.make_async_copy(source, target, small_sems.at[index])
        for index, (source, target) in enumerate(
            (
                (quad_hbm, quad_ref),
                (spectral_hbm, spectral_ref),
            )
        )
    ]
    small[0].start()
    loads[0].start()
    loads[1].start()
    for copy in small[1:] + loads[2:]:
        copy.start()
    first = own_wave(waves_ref)
    tail[...] = jnp.zeros_like(tail)
    weight_high, weight_low = split(remap_matrix(bounds_ref))
    weights = jnp.concatenate([weight_high, weight_high, weight_low], axis=1)
    degree, _ = row_layout(first, lax.broadcasted_iota(jnp.int32, (1, ROWS_PAD), 1))
    strength = column(diffusion_ref, (LEV, 128))
    for start in range(0, ROWS_PAD, 128):
        rows = slice(start, start + 128)
        scaled = 0.1 + degree[:, rows] * (degree[:, rows] + 1.0) / (NTRUNC * (NTRUNC + 1.0))
        rate = strength * scaled
        decay = jnp.exp(-rate)
        decay_ref[:, rows] = decay
        gain_ref[:, rows] = mean_decay(rate, decay)
    small[0].wait()

    def latitudes(group):
        rows = [received_ref[(4 * group + q) * LEV : (4 * group + q + 1) * LEV, :] for q in range(4)]
        return jnp.concatenate(regroup(rows), axis=0)

    for group in range(HALF // 128):
        cols = slice(128 * group, 128 * group + 128)
        north = latitudes(group)
        south = mirrored(latitudes(15 - group))
        weight = quad_ref[:, cols]
        for parity, value in ((0, weight * (north + south)), (1, weight * (north - south))):
            high, low = split(value)
            folded[64 * parity : 64 * parity + 64, cols] = high
            folded[128 + 64 * parity : 192 + 64 * parity, cols] = low

    for index, start in enumerate(CHUNKS[:-1]):
        stop = CHUNKS[index + 1]
        rows = slice(start, stop)
        row = start + lax.broadcasted_iota(jnp.int32, (1, stop - start), 1)
        _, combination = row_layout(first, row)
        loads[2 * index].wait()
        loads[2 * index + 1].wait()
        products = mxu(folded[...], panel_high[rows, :], NT) + mxu(folded[...], panel_low[rows, :], NT)
        products = products[:128] + products[128:]
        forcing = products[96:]
        for group in range(3):
            forcing = jnp.where(combination == group, products[32 * group : 32 * group + 32], forcing)
        if index == 0:
            for copy in small[1:]:
                copy.wait()
            tail[:, :1] = spectral_ref[:, ROWS - 1 :]
        decay = decay_ref[:, rows]
        gain = gain_ref[:, rows]
        state = spectral_ref[:, start : min(stop, ROWS - 1)]
        if stop > ROWS:
            state = jnp.concatenate([state, tail[...]], axis=1)
        advanced = (
            jnp.concatenate([decay, decay], axis=0) * state
            + jnp.concatenate([gain, gain], axis=0) * forcing
        )
        stop = min(stop, ROWS)
        new_ref[:, start:stop] = advanced[:, : stop - start]
        high, low = split(advanced)
        mixed = mxu(weights, jnp.concatenate([high, low, high], axis=0), NN)
        for part, value in enumerate(split(mixed)):
            zero = jnp.zeros_like(value)
            for group in range(4):
                place = slice(128 * part + 32 * group, 128 * part + 32 * group + 32)
                spread[place, rows] = jnp.where(combination == group, value, zero)
    store_new = pltpu.make_async_copy(new_ref, new_hbm, small_sems.at[2])
    store_new.start()
    total = mxu(spread[...], panel_high[...], NN)
    total = total[:128] + total[128:] + mxu(spread[:128], panel_low[...], NN)

    slot = lax.broadcasted_iota(jnp.int32, (64, 128), 0) // (2 * LEV)
    scale = jnp.where((slot == 0) & (first == 0), 1.0, 2.0) / math.sqrt(NLON)

    def store(group, value):
        parts = regroup([value[LEV * part : LEV * part + LEV] for part in range(4)])
        for q in range(4):
            out_ref[(4 * group + q) * LEV : (4 * group + q + 1) * LEV, :] = parts[q]

    for group in range(HALF // 128):
        cols = slice(128 * group, 128 * group + 128)
        even = total[:64, cols] * scale
        odd = total[64:, cols] * scale
        store(group, even + odd)
        store(15 - group, mirrored(even - odd))
    store_new.wait()


def legendre(waves, bounds, diffusion, received, prepared, spectral, quad_weights):
    high, low = prepared
    vmem = pl.BlockSpec(memory_space=pltpu.VMEM)
    smem = pl.BlockSpec(memory_space=pltpu.SMEM)
    anywhere = pl.BlockSpec(memory_space=pl.ANY)
    return pl.pallas_call(
        legendre_kernel,
        in_specs=[smem, smem, smem, vmem] + [anywhere] * 4,
        out_specs=[anywhere, vmem],
        out_shape=[
            jax.ShapeDtypeStruct((2 * LEV, ROWS), jnp.float32),
            jax.ShapeDtypeStruct((4 * PAIRS, 128), jnp.float32),
        ],
        scratch_shapes=[
            pltpu.VMEM((256, HALF), jnp.bfloat16),
            pltpu.VMEM((ROWS_PAD, HALF), jnp.bfloat16),
            pltpu.VMEM((ROWS_PAD, HALF), jnp.bfloat16),
            pltpu.VMEM((256, ROWS_PAD), jnp.bfloat16),
            pltpu.VMEM((2 * LEV, ROWS), jnp.float32),
            pltpu.VMEM((1, HALF), jnp.float32),
            pltpu.VMEM((LEV, ROWS_PAD), jnp.float32),
            pltpu.VMEM((LEV, ROWS_PAD), jnp.float32),
            pltpu.VMEM((2 * LEV, 128), jnp.float32),
            pltpu.VMEM((2 * LEV, ROWS), jnp.float32),
            pltpu.SemaphoreType.DMA((len(CHUNKS) - 1, 2)),
            pltpu.SemaphoreType.DMA((3,)),
        ],
        compiler_params=pltpu.CompilerParams(vmem_limit_bytes=VMEM_LEGENDRE),
        name="legendre",
    )(waves, bounds, diffusion, received, high, low, spectral, quad_weights)


def inverse_kernel(
    waves_hbm, received_ref, table, out_hbm, waves_ref, turned, grid, load_sems, store_sems
):
    count = len(LON_CUTS) - 1

    def target(index, part):
        start, stop = LON_CUTS[index], LON_CUTS[index + 1]
        begin = (start, FOLD - stop, FOLD + start, NLON - stop)[part]
        return slice(begin, begin + stop - start)

    def store(index, part):
        cols = target(index, part)
        cols = pl.ds(cols.start, cols.stop - cols.start)
        return pltpu.make_async_copy(grid.at[:, cols], out_hbm.at[:, cols], store_sems.at[index, part])

    load_waves = pltpu.make_async_copy(waves_hbm, waves_ref, load_sems.at[2])
    load_waves.start()
    parts = regroup([received_ref[pl.ds(level, PAIRS, stride=4), :] for level in range(4)])
    load_waves.wait()
    waves = wave_columns(waves_ref)
    for parity in range(2):
        half_cos, half_sin = cos_sin(waves[parity])
        real, imag = parts[2 * parity], parts[2 * parity + 1]
        for component, value in (
            (0, real * half_cos + imag * half_sin),
            (1, imag * half_cos - real * half_sin),
        ):
            high, low = split(value.T)
            for copy in range(2):
                cols = slice(PAIRS * copy, PAIRS * copy + PAIRS)
                turned[parity, component, :128, cols] = high
                turned[parity, component, 128:, cols] = low
    for index in range(count):
        cols = slice(LON_CUTS[index], LON_CUTS[index + 1])
        near, far = [], []
        for parity in range(2):
            sums = []
            for component in range(2):
                right = table[parity, component, :, :, cols].reshape(2 * PAIRS, cols.stop - cols.start)
                product = mxu(turned[parity, component], right, NN)
                sums.append(product[:128] + product[128:])
            near.append(sums[0] + sums[1])
            far.append(sums[parity] - sums[1 - parity])
        for part, value in enumerate(
            (
                near[0] + near[1],
                mirrored_wide(far[0] + far[1]),
                near[0] - near[1],
                mirrored_wide(far[0] - far[1]),
            )
        ):
            grid[:, target(index, part)] = value
            store(index, part).start()
    for index in range(count):
        for part in range(4):
            store(index, part).wait()


def inverse(waves, received, table):
    vmem = pl.BlockSpec(memory_space=pltpu.VMEM)
    return pl.pallas_call(
        inverse_kernel,
        in_specs=[pl.BlockSpec(memory_space=pl.ANY), vmem, vmem],
        out_specs=pl.BlockSpec(memory_space=pl.ANY),
        out_shape=jax.ShapeDtypeStruct((128, NLON), jnp.float32),
        scratch_shapes=[
            pltpu.VMEM((PAIRS // 128, 128), jnp.int32),
            pltpu.VMEM((2, 2, 256, 2 * PAIRS), jnp.bfloat16),
            pltpu.VMEM((128, NLON), jnp.float32),
            pltpu.SemaphoreType.DMA((3,)),
            pltpu.SemaphoreType.DMA((len(LON_CUTS) - 1, 4)),
        ],
        compiler_params=pltpu.CompilerParams(vmem_limit_bytes=VMEM_INVERSE),
        name="inverse",
    )(waves, received, table)


def exchange(block):
    moved = lax.all_to_all(block.reshape(PAIRS, 4, 128), ("lat", "lev"), 0, 0, tiled=True)
    return moved.reshape(4 * PAIRS, 128)


def body(tendency, spectral, panel, quad_weights, diffusion, waves, bounds):
    wave_rows = waves.reshape(PAIRS // 128, 128)
    coeffs, table = forward(wave_rows, tendency.reshape(128, NLON))
    advanced, returned = legendre(
        waves,
        bounds.T,
        diffusion,
        exchange(coeffs),
        prepare(panel.reshape(8 * ROWS, 128)),
        spectral.reshape(2 * LEV, ROWS),
        quad_weights[None, :],
    )
    grid = inverse(wave_rows, exchange(returned), table)
    return (grid.reshape(tendency.shape), advanced.reshape(spectral.shape))


def solution(mesh):
    return jax.shard_map(
        body,
        mesh=mesh,
        in_specs=(
            P("lev", "lat", None),
            P(("lat", "lev"), None, None, None),
            P(("lat", "lev"), None, None),
            P(),
            P(),
            P(),
            P(),
        ),
        out_specs=(P("lev", "lat", None), P(("lat", "lev"), None, None, None)),
        check_vma=False,
    )
```

```python
import math

import jax
import jax.numpy as jnp
from jax import lax
from jax.experimental import pallas as pl
from jax.experimental.pallas import tpu as pltpu
from jax.sharding import PartitionSpec as P

NTRUNC = 2048
SUBDIV = 8
NLON = 4096
TURN = 2 * NLON
FOLD = NLON // 2
QUARTER = NLON // 4
PAIRS = 256
ROWS = 2049
HALF = 1024
LEV = 16
ROW_BLOCK = 512
ROWS_PAD = 2176
CHUNKS = (0, 1024, ROWS_PAD)
LON_CUTS = (0, 512, 768, 1024)
VMEM = 58 * 1024 * 1024
VMEM_LEGENDRE = 52 * 1024 * 1024
VMEM_INVERSE = 48 * 1024 * 1024
NT = (((1,), (1,)), ((), ()))
NN = (((1,), (0,)), ((), ()))


def split(value):
    high = value.astype(jnp.bfloat16)
    low = (value - high.astype(jnp.float32)).astype(jnp.bfloat16)
    return (high, low)


def mxu(left, right, dims):
    return lax.dot_general(left, right, dims, preferred_element_type=jnp.float32)


def regroup(parts):
    return [
        jnp.concatenate([part[:, 32 * group : 32 * group + 32] for part in parts], axis=1)
        for group in range(4)
    ]


def cos_sin(turns):
    quadrant = (turns + TURN // 8) >> 11
    angle = (turns - (quadrant << 11)).astype(jnp.float32) * (2.0 * math.pi / TURN)
    sq = angle * angle
    sin = angle * (
        1.0 + sq * (-1.0 / 6 + sq * (1.0 / 120 + sq * (-1.0 / 5040 + sq * (1.0 / 362880))))
    )
    cos = 1.0 + sq * (
        -0.5 + sq * (1.0 / 24 + sq * (-1.0 / 720 + sq * (1.0 / 40320 + sq * (-1.0 / 3628800))))
    )
    swap = (quadrant & 1) == 1
    first = jnp.where(swap, sin, cos)
    second = jnp.where(swap, cos, sin)
    turned = quadrant & 3
    cos_out = jnp.where((turned == 1) | (turned == 2), -first, first)
    sin_out = jnp.where(turned >= 2, -second, second)
    return (cos_out, sin_out)


def mirrored(block):
    lane = lax.broadcasted_iota(jnp.int32, block.shape, 1)
    return jnp.take_along_axis(block, 127 - lane, axis=1)


def mirrored_wide(block):
    width = block.shape[1]
    parts = [mirrored(block[:, start - 128 : start]) for start in range(width, 0, -128)]
    return jnp.concatenate(parts, axis=1)


def wave_columns(waves_ref):
    halves = []
    for half in range(PAIRS // 128):
        row = waves_ref[half : half + 1, :].astype(jnp.float32)
        halves.append(jnp.broadcast_to(row, (128, 128)).T.astype(jnp.int32))
    wave = jnp.concatenate(halves, axis=0)
    even = jnp.where((wave & 1) == 1, NTRUNC - 1 - wave, wave)
    return (even, NTRUNC - 1 - even)


def mean_decay(rate, decay):
    series = jnp.full_like(rate, 1.0 / math.factorial(11))
    for order in range(10, 0, -1):
        series = 1.0 / math.factorial(order) - rate * series
    return jnp.where(rate < 1.0, series, (1.0 - decay) / rate)


def forward_kernel(
    waves_hbm, field_hbm, out_ref, table_hbm, waves_ref, field, folded, table, sems
):
    load = pltpu.make_async_copy(field_hbm, field, sems.at[3])
    load_waves = pltpu.make_async_copy(waves_hbm, waves_ref, sems.at[2])
    load_waves.start()
    load.start()
    load_waves.wait()
    waves = wave_columns(waves_ref)
    lane = lax.broadcasted_iota(jnp.int32, (32, 128), 1)
    half_steps = [[], []]

    def build(parity):
        for start in range(0, PAIRS, 32):
            rows = slice(start, start + 32)
            wave = waves[parity][rows]
            half_cos, half_sin = cos_sin(wave)
            half_steps[parity].append((half_cos, half_sin))
            cos, sin = cos_sin((wave * (2 * lane + 1)) & (TURN - 1))
            last_cos = jnp.broadcast_to(cos[:, 127:], cos.shape)
            last_sin = jnp.broadcast_to(sin[:, 127:], sin.shape)
            turn_cos = last_cos * half_cos - last_sin * half_sin
            turn_sin = last_sin * half_cos + last_cos * half_sin
            for block in range(QUARTER // 128):
                cols = slice(block * 128, block * 128 + 128)
                for component, value in ((0, cos), (1, -sin)):
                    high, low = split(value)
                    table[parity, component, 0, rows, cols] = high
                    table[parity, component, 1, rows, cols] = low
                cos, sin = (cos * turn_cos - sin * turn_sin, sin * turn_cos + cos * turn_sin)

    def store(parity):
        return pltpu.make_async_copy(table.at[parity], table_hbm.at[parity], sems.at[parity])

    for parity in range(2):
        build(parity)
        store(parity).start()
    load.wait()
    parts = []
    for parity in range(2):
        for start in range(0, QUARTER, 128):
            near = slice(start, start + 128)
            head, tail = field[:, near], field[:, FOLD - 128 - start : FOLD - start]
            east_head = field[:, start + FOLD : start + FOLD + 128]
            east_tail = field[:, NLON - 128 - start : NLON - start]
            if parity == 0:
                head, tail = head + east_head, tail + east_tail
            else:
                head, tail = head - east_head, tail - east_tail
            tail = mirrored(tail)
            for component, value in ((parity, head + tail), (1 - parity, head - tail)):
                high, low = split(value)
                folded[parity, component, :128, near] = high
                folded[parity, component, 128:, near] = low
        sums = []
        for component in range(2):
            left = table[parity, component].reshape(2 * PAIRS, QUARTER)
            product = mxu(left, folded[parity, component], NT)
            product = product[:, :128] + product[:, 128:]
            sums.append((product[:PAIRS] + product[PAIRS:]) * (1.0 / math.sqrt(NLON)))
        half_cos = jnp.concatenate([item[0] for item in half_steps[parity]], axis=0)
        half_sin = jnp.concatenate([item[1] for item in half_steps[parity]], axis=0)
        parts += [sums[0] * half_cos - sums[1] * half_sin, sums[0] * half_sin + sums[1] * half_cos]
    for level, value in enumerate(regroup(parts)):
        out_ref[pl.ds(level, PAIRS, stride=4), :] = value
    for parity in range(2):
        store(parity).wait()


def forward(waves, field):
    return pl.pallas_call(
        forward_kernel,
        in_specs=[pl.BlockSpec(memory_space=pl.ANY)] * 2,
        out_specs=[pl.BlockSpec(memory_space=pltpu.VMEM), pl.BlockSpec(memory_space=pl.ANY)],
        out_shape=[
            jax.ShapeDtypeStruct((4 * PAIRS, 128), jnp.float32),
            jax.ShapeDtypeStruct((2, 2, 2, PAIRS, QUARTER), jnp.bfloat16),
        ],
        scratch_shapes=[
            pltpu.VMEM((PAIRS // 128, 128), jnp.int32),
            pltpu.VMEM((128, NLON), jnp.float32),
            pltpu.VMEM((2, 2, 256, QUARTER), jnp.bfloat16),
            pltpu.VMEM((2, 2, 2, PAIRS, QUARTER), jnp.bfloat16),
            pltpu.SemaphoreType.DMA((4,)),
        ],
        compiler_params=pltpu.CompilerParams(vmem_limit_bytes=VMEM),
        name="forward",
    )(waves, field)


def row_layout(first, row):
    leading = row < NTRUNC - first
    degree = jnp.where(leading, first + row, row - 1).astype(jnp.float32)
    parity = jnp.where(leading, row, row + first) & 1
    slot = jnp.where(leading, first & 1, 1 - (first & 1))
    return (degree, 2 * parity + slot)


def own_wave(waves_ref):
    return waves_ref[lax.axis_index("lat") * lax.axis_size("lev") + lax.axis_index("lev")]


def column(values_ref, shape):
    row = lax.broadcasted_iota(jnp.int32, shape, 0) % LEV
    result = jnp.full(shape, values_ref[0])
    for index in range(1, LEV):
        result = jnp.where(row == index, values_ref[index], result)
    return result


def prepare_kernel(panel_ref, high_ref, low_ref):
    step = pl.program_id(0)
    last = ROWS // ROW_BLOCK

    def divide(rows, keep):
        for chunk in range(8):
            cols = slice(128 * chunk, 128 * chunk + 128)
            high, low = split(keep(panel_ref[pl.ds(chunk, rows, stride=8), :]))
            high_ref[:rows, cols] = high
            low_ref[:rows, cols] = low

    @pl.when(step < last)
    def _():
        divide(ROW_BLOCK, lambda value: value)

    @pl.when(step == last)
    def _():
        rows = ROWS_PAD - last * ROW_BLOCK
        inside = lax.broadcasted_iota(jnp.int32, (rows, 128), 0) < ROWS - last * ROW_BLOCK
        divide(rows, lambda value: jnp.where(inside, value, 0.0))


def prepare(panel):
    by_rows = pl.BlockSpec((ROW_BLOCK, HALF), lambda i: (i, 0))
    return pl.pallas_call(
        prepare_kernel,
        grid=(ROWS // ROW_BLOCK + 1,),
        in_specs=[pl.BlockSpec((8 * ROW_BLOCK, 128), lambda i: (i, 0))],
        out_specs=[by_rows, by_rows],
        out_shape=[
            jax.ShapeDtypeStruct((ROWS_PAD, HALF), jnp.bfloat16),
            jax.ShapeDtypeStruct((ROWS_PAD, HALF), jnp.bfloat16),
        ],
        compiler_params=pltpu.CompilerParams(vmem_limit_bytes=VMEM),
        cost_estimate=pl.CostEstimate(flops=20_000_000, bytes_accessed=18_000_000, transcendentals=0),
        name="prepare",
    )(panel)


def remap_matrix(bounds_ref):
    shape = (2 * LEV, 2 * LEV)
    target = lax.broadcasted_iota(jnp.int32, shape, 0)
    source = lax.broadcasted_iota(jnp.int32, shape, 1)
    lower = column(bounds_ref.at[0], shape)
    upper = column(bounds_ref.at[1], shape)
    level = source % LEV
    crossing = jnp.minimum(upper, (level + 1) * SUBDIV) - jnp.maximum(lower, level * SUBDIV)
    crossing = jnp.where(target // LEV == source // LEV, jnp.maximum(crossing, 0), 0)
    return crossing.astype(jnp.float32) / (upper - lower).astype(jnp.float32)


def legendre_kernel(
    waves_ref,
    bounds_ref,
    diffusion_ref,
    received_ref,
    high_hbm,
    low_hbm,
    spectral_hbm,
    quad_hbm,
    new_hbm,
    out_ref,
    folded,
    panel_high,
    panel_low,
    spread,
    spectral_ref,
    quad_ref,
    decay_ref,
    gain_ref,
    tail,
    new_ref,
    sems,
    small_sems,
):
    loads = []
    for index, start in enumerate(CHUNKS[:-1]):
        rows = pl.ds(start, CHUNKS[index + 1] - start)
        for kind, (source, target) in enumerate(((high_hbm, panel_high), (low_hbm, panel_low))):
            loads.append(
                pltpu.make_async_copy(source.at[rows, :], target.at[rows, :], sems.at[index, kind])
            )
    small = [
        pltpu.make_async_copy(source, target, small_sems.at[index])
        for index, (source, target) in enumerate(
            (
                (quad_hbm, quad_ref),
                (spectral_hbm, spectral_ref),
            )
        )
    ]
    small[0].start()
    loads[0].start()
    loads[1].start()
    for copy in small[1:] + loads[2:]:
        copy.start()
    first = own_wave(waves_ref)
    tail[...] = jnp.zeros_like(tail)
    weight_high, weight_low = split(remap_matrix(bounds_ref))
    weights = jnp.concatenate([weight_high, weight_high, weight_low], axis=1)
    degree, _ = row_layout(first, lax.broadcasted_iota(jnp.int32, (1, ROWS_PAD), 1))
    strength = column(diffusion_ref, (LEV, 128))
    for start in range(0, ROWS_PAD, 128):
        rows = slice(start, start + 128)
        scaled = 0.1 + degree[:, rows] * (degree[:, rows] + 1.0) / (NTRUNC * (NTRUNC + 1.0))
        rate = strength * scaled
        decay = jnp.exp(-rate)
        decay_ref[:, rows] = decay
        gain_ref[:, rows] = mean_decay(rate, decay)
    small[0].wait()

    def latitudes(group):
        rows = [received_ref[(4 * group + q) * LEV : (4 * group + q + 1) * LEV, :] for q in range(4)]
        return jnp.concatenate(regroup(rows), axis=0)

    for group in range(HALF // 128):
        cols = slice(128 * group, 128 * group + 128)
        north = latitudes(group)
        south = mirrored(latitudes(15 - group))
        weight = quad_ref[:, cols]
        for parity, value in ((0, weight * (north + south)), (1, weight * (north - south))):
            high, low = split(value)
            folded[64 * parity : 64 * parity + 64, cols] = high
            folded[128 + 64 * parity : 192 + 64 * parity, cols] = low

    for index, start in enumerate(CHUNKS[:-1]):
        stop = CHUNKS[index + 1]
        rows = slice(start, stop)
        row = start + lax.broadcasted_iota(jnp.int32, (1, stop - start), 1)
        _, combination = row_layout(first, row)
        loads[2 * index].wait()
        loads[2 * index + 1].wait()
        products = mxu(folded[...], panel_high[rows, :], NT) + mxu(folded[...], panel_low[rows, :], NT)
        products = products[:128] + products[128:]
        forcing = products[96:]
        for group in range(3):
            forcing = jnp.where(combination == group, products[32 * group : 32 * group + 32], forcing)
        if index == 0:
            for copy in small[1:]:
                copy.wait()
            tail[:, :1] = spectral_ref[:, ROWS - 1 :]
        decay = decay_ref[:, rows]
        gain = gain_ref[:, rows]
        state = spectral_ref[:, start : min(stop, ROWS - 1)]
        if stop > ROWS:
            state = jnp.concatenate([state, tail[...]], axis=1)
        advanced = (
            jnp.concatenate([decay, decay], axis=0) * state
            + jnp.concatenate([gain, gain], axis=0) * forcing
        )
        stop = min(stop, ROWS)
        new_ref[:, start:stop] = advanced[:, : stop - start]
        high, low = split(advanced)
        mixed = mxu(weights, jnp.concatenate([high, low, high], axis=0), NN)
        for part, value in enumerate(split(mixed)):
            zero = jnp.zeros_like(value)
            for group in range(4):
                place = slice(128 * part + 32 * group, 128 * part + 32 * group + 32)
                spread[place, rows] = jnp.where(combination == group, value, zero)
    store_new = pltpu.make_async_copy(new_ref, new_hbm, small_sems.at[2])
    store_new.start()
    total = mxu(spread[...], panel_high[...], NN)
    total = total[:128] + total[128:] + mxu(spread[:128], panel_low[...], NN)

    slot = lax.broadcasted_iota(jnp.int32, (64, 128), 0) // (2 * LEV)
    scale = jnp.where((slot == 0) & (first == 0), 1.0, 2.0) / math.sqrt(NLON)

    def store(group, value):
        parts = regroup([value[LEV * part : LEV * part + LEV] for part in range(4)])
        for q in range(4):
            out_ref[(4 * group + q) * LEV : (4 * group + q + 1) * LEV, :] = parts[q]

    for group in range(HALF // 128):
        cols = slice(128 * group, 128 * group + 128)
        even = total[:64, cols] * scale
        odd = total[64:, cols] * scale
        store(group, even + odd)
        store(15 - group, mirrored(even - odd))
    store_new.wait()


def legendre(waves, bounds, diffusion, received, prepared, spectral, quad_weights):
    high, low = prepared
    vmem = pl.BlockSpec(memory_space=pltpu.VMEM)
    smem = pl.BlockSpec(memory_space=pltpu.SMEM)
    anywhere = pl.BlockSpec(memory_space=pl.ANY)
    return pl.pallas_call(
        legendre_kernel,
        in_specs=[smem, smem, smem, vmem] + [anywhere] * 4,
        out_specs=[anywhere, vmem],
        out_shape=[
            jax.ShapeDtypeStruct((2 * LEV, ROWS), jnp.float32),
            jax.ShapeDtypeStruct((4 * PAIRS, 128), jnp.float32),
        ],
        scratch_shapes=[
            pltpu.VMEM((256, HALF), jnp.bfloat16),
            pltpu.VMEM((ROWS_PAD, HALF), jnp.bfloat16),
            pltpu.VMEM((ROWS_PAD, HALF), jnp.bfloat16),
            pltpu.VMEM((256, ROWS_PAD), jnp.bfloat16),
            pltpu.VMEM((2 * LEV, ROWS), jnp.float32),
            pltpu.VMEM((1, HALF), jnp.float32),
            pltpu.VMEM((LEV, ROWS_PAD), jnp.float32),
            pltpu.VMEM((LEV, ROWS_PAD), jnp.float32),
            pltpu.VMEM((2 * LEV, 128), jnp.float32),
            pltpu.VMEM((2 * LEV, ROWS), jnp.float32),
            pltpu.SemaphoreType.DMA((len(CHUNKS) - 1, 2)),
            pltpu.SemaphoreType.DMA((3,)),
        ],
        compiler_params=pltpu.CompilerParams(vmem_limit_bytes=VMEM_LEGENDRE),
        name="legendre",
    )(waves, bounds, diffusion, received, high, low, spectral, quad_weights)


def inverse_kernel(
    waves_ref, received_ref, table, out_hbm, turned, grid, store_sems
):
    count = len(LON_CUTS) - 1

    def target(index, part):
        start, stop = LON_CUTS[index], LON_CUTS[index + 1]
        begin = (start, FOLD - stop, FOLD + start, NLON - stop)[part]
        return slice(begin, begin + stop - start)

    def store(index, part):
        cols = target(index, part)
        cols = pl.ds(cols.start, cols.stop - cols.start)
        return pltpu.make_async_copy(grid.at[:, cols], out_hbm.at[:, cols], store_sems.at[index, part])

    parts = regroup([received_ref[pl.ds(level, PAIRS, stride=4), :] for level in range(4)])
    waves = wave_columns(waves_ref)
    for parity in range(2):
        half_cos, half_sin = cos_sin(waves[parity])
        real, imag = parts[2 * parity], parts[2 * parity + 1]
        for component, value in (
            (0, real * half_cos + imag * half_sin),
            (1, imag * half_cos - real * half_sin),
        ):
            high, low = split(value.T)
            for copy in range(2):
                cols = slice(PAIRS * copy, PAIRS * copy + PAIRS)
                turned[parity, component, :128, cols] = high
                turned[parity, component, 128:, cols] = low
    for index in range(count):
        cols = slice(LON_CUTS[index], LON_CUTS[index + 1])
        near, far = [], []
        for parity in range(2):
            sums = []
            for component in range(2):
                right = table[parity, component, :, :, cols].reshape(2 * PAIRS, cols.stop - cols.start)
                product = mxu(turned[parity, component], right, NN)
                sums.append(product[:128] + product[128:])
            near.append(sums[0] + sums[1])
            far.append(sums[parity] - sums[1 - parity])
        for part, value in enumerate(
            (
                near[0] + near[1],
                mirrored_wide(far[0] + far[1]),
                near[0] - near[1],
                mirrored_wide(far[0] - far[1]),
            )
        ):
            grid[:, target(index, part)] = value
            store(index, part).start()
    for index in range(count):
        for part in range(4):
            store(index, part).wait()


def inverse(waves, received, table):
    vmem = pl.BlockSpec(memory_space=pltpu.VMEM)
    return pl.pallas_call(
        inverse_kernel,
        in_specs=[vmem, vmem, vmem],
        out_specs=pl.BlockSpec(memory_space=pl.ANY),
        out_shape=jax.ShapeDtypeStruct((128, NLON), jnp.float32),
        scratch_shapes=[
            pltpu.VMEM((2, 2, 256, 2 * PAIRS), jnp.bfloat16),
            pltpu.VMEM((128, NLON), jnp.float32),
            pltpu.SemaphoreType.DMA((len(LON_CUTS) - 1, 4)),
        ],
        compiler_params=pltpu.CompilerParams(vmem_limit_bytes=VMEM_INVERSE),
        name="inverse",
    )(waves, received, table)


def exchange(block):
    moved = lax.all_to_all(block.reshape(PAIRS, 4, 128), ("lat", "lev"), 0, 0, tiled=True)
    return moved.reshape(4 * PAIRS, 128)


def body(tendency, spectral, panel, quad_weights, diffusion, waves, bounds):
    wave_rows = waves.reshape(PAIRS // 128, 128)
    coeffs, table = forward(wave_rows, tendency.reshape(128, NLON))
    advanced, returned = legendre(
        waves,
        bounds.T,
        diffusion,
        exchange(coeffs),
        prepare(panel.reshape(8 * ROWS, 128)),
        spectral.reshape(2 * LEV, ROWS),
        quad_weights[None, :],
    )
    grid = inverse(wave_rows, exchange(returned), table)
    return (grid.reshape(tendency.shape), advanced.reshape(spectral.shape))


def solution(mesh):
    return jax.shard_map(
        body,
        mesh=mesh,
        in_specs=(
            P("lev", "lat", None),
            P(("lat", "lev"), None, None, None),
            P(("lat", "lev"), None, None),
            P(),
            P(),
            P(),
            P(),
        ),
        out_specs=(P("lev", "lat", None), P(("lat", "lev"), None, None, None)),
        check_vma=False,
    )
```
